32 devices in a mesh: br: 16 (over z, y, x), bus: 2 (over core).
Axes of the slice: x: 2, y: 2, z: 4, core: 2. Of those that a mesh axis runs over, the one named last changes fastest.
Arguments:
- shift_factors: bfloat16 [12288, 20480], P('br', 'bus'), may hold values from -0.0625 to 0.0625
- injections: bfloat16 [20480, 128], P(('bus', 'br')), may hold values from -6 to 6
- limits: float32 [12288], P(('br', 'bus')), may hold values from 0.2 to 2
- entry_row: int32 [16384], P(('br', 'bus')), may hold values from 0 to 383
- entry_owner: int32 [16384, 1], P(('br', 'bus')), may hold values from 0 to 15; in each aligned block of 512 rows (0 to 511, 512 to 1023, ...) at most 64 rows name the same one
- entry_slot: int32 [16384], P(('br', 'bus')), may hold values from 0 to 7
- outage_factor: float32 [16384], P(('br', 'bus')), may hold values from -1 to 1
- outage_row: int32 [128], P(('br', 'bus')), may hold values from 0 to 383
Outputs:
- injection_grad: float32 [20480, 128], P(('bus', 'br'))
The draws below stay inside these ranges and needn't reach their ends.
Inputs may be any that keep to these rules, and one draw needn't show every extreme that they name: `entry_owner`: among the pairs of one device no owner appears more than 64 times, and in every draw some device names some owner exactly 64 times.
All inputs are finite; a program needn't handle non-finite values.
Results may differ from the reference program's by a relative error of at most 0.0016.
The reference program's roundings to bfloat16 on the way (of `adjoint`) count: a program that leaves them out, or rounds other values in their place, can miss the bound.
Values may be sent and summed in bfloat16 or wider, within the bound.
No kernel may reach another device: no remote copies, remote signals or barrier semaphores. Data moves between devices by JAX's collectives and lax.ppermute only.
A program may use at most 64 MiB of HBM per device.

```python
import math
import jax
import jax.numpy as jnp
import numpy as np
from jax import lax

BUSES = 20480
SCENARIOS = 128
CONT_DEV = 4
ENTRY_DEV = 512
ROWS_DEV = 384
BRANCHES = 12288
GROUP_CONTS = 8
CONTINGENCIES = 128
ENTRIES = 16384
CAPACITY = 64
N_BR = 16


def with_ends(drawn, own_key, smallest, top_value):
    dims = drawn.shape
    place = [jax.random.randint(jax.random.fold_in(own_key, axis), (), 0, dims[axis]) for axis in range(len(dims))]
    drawn = drawn.at[tuple(place)].set(smallest)
    longest = dims.index(max(dims))
    place[longest] = (place[longest] + 1) % dims[longest]
    return drawn.at[tuple(place)].set(top_value)


def with_spikes(array, key, source, target, parts, factor):
    owner, partner = [(jnp.arange(array.shape[axis_at]) // (array.shape[axis_at] // parts)).reshape([-1 if axis == axis_at else 1 for axis in range(array.ndim)]) for axis_at in (source, target)]
    chosen = jax.random.permutation(key, parts)[partner]
    strong = (owner == chosen) | (owner == (partner + parts // 2) % parts)
    return jnp.where(strong, factor * array, array)


def shard_levels(key, shape, pieces, smallest, largest):
    level, own = 1.0, jax.random.fold_in(key, 6)
    for dim, blocks in pieces:
        draws = jnp.exp(jax.random.uniform(jax.random.fold_in(own, dim), (blocks,), jnp.float32, smallest / len(pieces), largest / len(pieces)))
        level = level * jnp.repeat(draws, shape[dim] // blocks).reshape([-1 if axis == dim else 1 for axis in range(len(shape))])
    return level


def shared_out(rng, own, number, rows, amount, top, limit, skew):
    sequence = jax.random.permutation(rng, amount)
    heavy_load, common = portions_of(amount, rows * top, limit, skew, True), portions_of(amount, rows * top, limit, skew, False)
    places = jnp.arange(amount)

    def named(tallies, rotation):
        used = int((tallies > 0).sum())
        fixed = max(1, used // 4)
        shifted = fixed + (places - fixed + rotation * (used - fixed)) % max(1, amount - fixed)
        return jnp.zeros((amount,), jnp.int32).at[sequence[jnp.where(places < fixed, places, shifted)]].set(jnp.asarray(tallies, jnp.int32))

    tallies = jnp.where(number % 4 == 0, named(heavy_load, number // 4), named(common, number - number // 4 - 1))
    mixed = jax.random.permutation(jax.random.fold_in(own, 3), amount)
    giver, taker = mixed[0:amount // 2 * 2:2], mixed[1:amount // 2 * 2:2]
    slack = jnp.minimum(tallies[giver] - 1, limit - tallies[taker]) // 2
    slack = jnp.where((giver == sequence[0]) | (taker == sequence[0]) | (tallies[taker] == 0), 0, jnp.maximum(slack, 0))
    shifted = jax.random.randint(jax.random.fold_in(own, 4), (amount // 2,), 0, 1 << 20) % (slack + 1)
    tallies = tallies.at[giver].add(-shifted).at[taker].add(shifted)
    members = jnp.searchsorted(jnp.cumsum(tallies), jnp.arange(rows * top), side="right").astype(jnp.int32)
    table = members.reshape(top, rows).T
    table = table[jax.random.permutation(jax.random.fold_in(own, 1), rows)]
    rotation = jax.random.randint(jax.random.fold_in(own, 2), (rows, 1), 0, top)
    return jnp.take_along_axis(table, (jnp.arange(top)[None, :] + rotation) % top, axis=1)


def portions_of(number_of, total, bound, lean, full):
    loads = [(1 << 20) // math.isqrt(grade ** lean) + 1 for grade in range(1, number_of + 1)]
    largest = bound if full else min(bound, max(-(-total // number_of), total * loads[0] // sum(loads)))
    least = 1 if total - largest >= number_of - 1 else 0
    counts, surplus = [largest] + [least] * (number_of - 1), total - largest - least * (number_of - 1)
    while surplus > 0:
        candidates = [i for i in range(1, number_of) if counts[i] < largest] or [i for i in range(1, number_of) if counts[i] < bound]
        mass, budget = sum([loads[i] for i in candidates]), surplus
        for i in candidates:
            more = min(bound - counts[i], max(1, budget * loads[i] // mass), surplus)
            counts[i] = counts[i] + more
            surplus = surplus - more
    return np.array(counts)


def noise(own_key, dims, scale, most, split=(), held_as=jnp.bfloat16):
    array = jax.random.normal(own_key, dims, jnp.float32) * scale
    if len(split) > 0:
        array = shard_levels(own_key, dims, split, -0.22, 0.18) * array
    return jnp.clip(array, min=-most, max=most).astype(held_as)


def bell_draw_with(own_key, dims, spread, most, split, heavy, kind=jnp.bfloat16):
    array = spread * jax.random.normal(own_key, dims, jnp.float32)
    if split:
        array = array * shard_levels(own_key, dims, split, -0.22, 0.18)
    return jnp.clip(with_spikes(array, jax.random.fold_in(own_key, 3), *heavy), -most, most).astype(kind)


def setup_inputs(seed: int = 0) -> dict:
    key_list = jax.random.split(jax.random.key(seed), 9)
    shift_factors = bell_draw_with(key_list[0], (BRANCHES, BUSES), BUSES ** -0.5, 0.0625, ((0, 16), (1, 2)), (0, 1, 16, 2.0))
    injections = noise(key_list[1], (BUSES, SCENARIOS), 1.0, 6.0, ((0, 32),))
    limits = jnp.clip(jnp.exp(math.log(2.0) - 2.3025851 * jax.random.uniform(key_list[2], (BRANCHES,), jnp.float32) ** shard_levels(key_list[2], (BRANCHES,), ((0, 32),), -0.2, 0.2)), 0.2, 2.0)
    entry_row = with_ends(jax.random.randint(key_list[3], (ENTRIES,), 0, ROWS_DEV), jax.random.fold_in(key_list[3], 1), 0, ROWS_DEV - 1).astype(jnp.int32)
    entry_owner_keys = jax.random.split(jax.random.fold_in(key_list[4], 1), ENTRIES // ENTRY_DEV)
    entry_owner_turns = jax.random.permutation(jax.random.fold_in(key_list[4], 3), ENTRIES // ENTRY_DEV)
    entry_owner = jax.vmap(lambda own, number: shared_out(jax.random.fold_in(key_list[4], 2), own, number, ENTRY_DEV, N_BR, 1, CAPACITY, 2))(entry_owner_keys, entry_owner_turns).reshape((ENTRIES, 1))
    entry_slot = with_ends(jax.random.randint(key_list[5], (ENTRIES,), 0, GROUP_CONTS), jax.random.fold_in(key_list[5], 1), 0, GROUP_CONTS - 1).astype(jnp.int32)
    outage_factor = jnp.clip(jax.random.uniform(key_list[6], (ENTRIES,), jnp.float32, -1.0, 1.0) * shard_levels(key_list[6], (ENTRIES,), ((0, 32),), -0.4, 0.0), -1.0, 1.0)
    outage_row = with_ends(jax.random.randint(key_list[7], (CONTINGENCIES,), 0, ROWS_DEV), jax.random.fold_in(key_list[7], 1), 0, ROWS_DEV - 1).astype(jnp.int32)
    return {"shift_factors": shift_factors, "injections": injections, "limits": limits, "entry_row": entry_row, "entry_owner": entry_owner, "entry_slot": entry_slot, "outage_factor": outage_factor, "outage_row": outage_row}


base_weight = 1.0
cont_weight = 0.25
emergency = 1.25


def reference(shift_factors, injections, limits, entry_row, entry_owner, entry_slot, outage_factor, outage_row):
    row_block = math.gcd(BRANCHES, 1024)
    factor_blocks = shift_factors.reshape(BRANCHES // row_block, row_block, BUSES)

    def forward_block(factor_rows):
        return jnp.dot(factor_rows, injections, preferred_element_type=jnp.float32)

    flows = lax.map(forward_block, factor_blocks).reshape(BRANCHES, SCENARIOS)
    limit_col = limits[:, None]
    base_adj = base_weight * (jnp.maximum(flows - limit_col, 0.0) + jnp.minimum(flows + limit_col, 0.0))
    device_of = jnp.arange(ENTRIES, dtype=jnp.int32) // ENTRY_DEV
    monitored = (device_of * ROWS_DEV + entry_row).astype(jnp.int32)
    contingency = (entry_owner[:, 0] * GROUP_CONTS + entry_slot).astype(jnp.int32)
    out_branch = ((jnp.arange(CONTINGENCIES, dtype=jnp.int32) // CONT_DEV) * ROWS_DEV + outage_row).astype(jnp.int32)
    outage = flows[out_branch]
    post_flow = flows[monitored] + outage_factor[:, None] * outage[contingency]
    emerg_cap = emergency * limits[monitored][:, None]
    entry_adj = cont_weight * (jnp.maximum(post_flow - emerg_cap, 0.0) + jnp.minimum(post_flow + emerg_cap, 0.0))
    outage_adj = jax.ops.segment_sum(outage_factor[:, None] * entry_adj, contingency, num_segments=CONTINGENCIES)
    adjoint = base_adj.at[monitored].add(entry_adj).at[out_branch].add(outage_adj)
    adjoint = adjoint.astype(jnp.bfloat16)
    adjoint_blocks = adjoint.reshape(BRANCHES // row_block, row_block, SCENARIOS)

    def backward_block(running, pair):
        factor_rows, adjoint_rows = pair
        update = lax.dot_general(factor_rows, adjoint_rows, (((0,), (0,)), ((), ())), preferred_element_type=jnp.float32)
        return running + update, None

    gradient, unused = lax.scan(backward_block, jnp.zeros((BUSES, SCENARIOS), jnp.float32), (factor_blocks, adjoint_blocks))
    return gradient
```

```python
import functools

import jax
import jax.numpy as jnp
from jax import lax
from jax.experimental import pallas as pl
from jax.experimental.pallas import tpu as pltpu
from jax.sharding import PartitionSpec as P

base_weight = 1.0
cont_weight = 0.25
emergency = 1.25

F32 = jnp.float32
BF16 = jnp.bfloat16
VM = pl.BlockSpec(memory_space=pltpu.VMEM)
SM = pl.BlockSpec(memory_space=pltpu.SMEM)
LEVELS = 32000.0
LANES = 128


def call(body, out_shape, in_specs, name, scratch=(), flops=0, nbytes=0, limit=24):
    many = isinstance(out_shape, (tuple, list))
    return pl.pallas_call(
        body,
        out_shape=out_shape,
        in_specs=in_specs,
        out_specs=[VM] * len(out_shape) if many else VM,
        scratch_shapes=list(scratch),
        compiler_params=pltpu.CompilerParams(vmem_limit_bytes=limit << 20),
        cost_estimate=pl.CostEstimate(flops=flops, bytes_accessed=nbytes, transcendentals=0),
        name=name,
    )


def sds(shape, dtype):
    return jax.ShapeDtypeStruct(shape, dtype)


def forward(factors, shards, places, plane, total, name, rows_out=None):
    rows = factors.shape[0]
    width, scen = shards[0].shape
    n = len(shards)
    scal = jnp.stack([plane, *places]).astype(jnp.int32)
    keep = total is not None

    def body(scal_ref, f_ref, *refs):
        ins, refs = refs[:n], refs[n:]
        tot_ref, refs = (refs[0], refs[1:]) if keep else (None, refs)
        out_ref, buf = refs
        for g in range(n):
            buf[pl.ds(pl.multiple_of(scal_ref[1 + g] * width, width), width), :] = ins[g][...]
        start = pl.multiple_of(scal_ref[0] * width, width)
        part = jnp.dot(f_ref[:, pl.ds(start, n * width)], buf[...], preferred_element_type=F32)
        out_ref[...] = part + tot_ref[...] if keep else part

    ops = [scal, factors, *shards] + ([total] if keep else [])
    return call(
        body,
        sds((rows, scen), F32),
        [SM] + [VM] * (len(ops) - 1),
        name,
        [pltpu.VMEM((n * width, scen), BF16)],
        flops=2 * rows * n * width * scen,
        nbytes=n * width * (rows + scen) * 2,
    )(*ops)


def put_coded(ref, blocks):
    width = blocks[0].shape[1]
    top = functools.reduce(
        jnp.maximum, [jnp.max(jnp.abs(b), axis=1, keepdims=True) for b in blocks]
    )
    power = jnp.ceil(jnp.log2(jnp.maximum(top, 1e-30)))
    scale = jnp.exp2(-power) * LEVELS
    for n, b in enumerate(blocks):
        ref[:, n * width : (n + 1) * width] = jnp.round(b * scale).astype(jnp.int32).astype(jnp.int16)
    end = len(blocks) * width
    ref[:, end:] = jnp.broadcast_to(power, (ref.shape[0], LANES)).astype(jnp.int32).astype(jnp.int16)


def get_coded(ref, n, width):
    power = ref[:, ref.shape[1] - LANES :].astype(jnp.int32).astype(F32)[:, :1]
    scale = jnp.exp2(power) * (1.0 / LEVELS)
    return ref[:, n * width : (n + 1) * width].astype(jnp.int32).astype(F32) * scale


def three(x):
    high = x.astype(BF16)
    rest = x - high.astype(F32)
    middle = rest.astype(BF16)
    low = (rest - middle.astype(F32)).astype(BF16)
    return jnp.concatenate([high, middle, low], axis=1)


def pick(hot, x):
    n = x.shape[1]
    y = jnp.dot(hot, three(x), preferred_element_type=F32)
    return y[:, :n] + y[:, n : 2 * n] + y[:, 2 * n :]


def one_hot(hit):
    return jnp.where(hit, 1.0, 0.0).astype(BF16)


def overload(x, cap):
    return jnp.maximum(x - cap, 0.0) + jnp.minimum(x + cap, 0.0)


def on_slice(
    shift_factors, injections, limits, entry_row, entry_owner, entry_slot, outage_factor, outage_row
):
    rows, cols = shift_factors.shape
    width, scen = injections.shape
    half = rows // 2
    pairs = entry_row.shape[0]
    owned = outage_row.shape[0]
    me = lax.axis_index("br")
    core = lax.axis_index("bus")
    zz, spot = me // 4, me % 4
    mid = (zz == 1) | (zz == 2)

    def index(z, y, x):
        return z * 4 + y * 2 + x

    chips = [(z, y, x) for z in range(4) for y in range(2) for x in range(2)]
    to_x = [(index(z, y, x), index(z, y, 1 - x)) for z, y, x in chips]
    to_y = [(index(z, y, x), index(z, 1 - y, x)) for z, y, x in chips]
    to_z = {k: [(index(z, y, x), index(z ^ k, y, x)) for z, y, x in chips] for k in (1, 2, 3)}
    inner = [(index(z, y, x), index(3 - z, y, x)) for z, y, x in chips if z in (1, 2)]
    outward = [(index(z, y, x), index(z ^ 1, y, x)) for z, y, x in chips if z in (1, 2)]

    def send(v, perm):
        return lax.ppermute(v, "br", perm)

    def swap(v):
        return lax.ppermute(v, "bus", [(0, 1), (1, 0)])

    own = injections
    pair = send(own, to_z[1])
    third_mid = send(own, inner)
    own_x, own_y = send(own, to_x), send(own, to_y)
    fourth_mid = send(pair, inner)
    third_end = send(third_mid, outward)
    pair_x, pair_y = send(pair, to_x), send(pair, to_y)
    fourth_end = send(fourth_mid, outward)
    third = jnp.where(mid, third_mid, third_end)
    fourth = jnp.where(mid, fourth_mid, fourth_end)
    third_x, third_y = send(third, to_x), send(third, to_y)
    own_d = send(own_y, to_x)
    pair_d = send(pair_x, to_y)
    third_d = send(third_y, to_x)
    fourth_x, fourth_y = send(fourth, to_x), send(fourth, to_y)
    fourth_d = send(fourth_x, to_y)
    low = zz < 2
    z_third = jnp.where(low, 2, 1)
    z_fourth = jnp.where(low, 3, 0)
    places = [spot, spot ^ 1, spot ^ 2, spot ^ 3]

    factors = pltpu.with_memory_space_constraint(shift_factors, pltpu.VMEM)
    part = forward(factors, [own, own_x, own_y, own_d], places, zz * 4, None, "forward_own")
    part = forward(factors, [pair, pair_x, pair_y, pair_d], places, (zz ^ 1) * 4, part, "forward_pair")
    part = forward(factors, [third, third_x, third_y, third_d], places, z_third * 4, part, "forward_third")
    part = forward(factors, [fourth, fourth_x, fourth_y, fourth_d], places, z_fourth * 4, part, "forward_fourth")

    mine = lax.dynamic_slice_in_dim(part, core * half, half, 0)
    theirs = lax.dynamic_slice_in_dim(part, (1 - core) * half, half, 0)
    flows = mine + swap(theirs)

    group = jnp.concatenate([lax.dynamic_slice_in_dim(flows, outage_row[t], 1, 0) for t in range(owned)], axis=0)
    group = jnp.concatenate([group, swap(group)], axis=0)
    group = jnp.concatenate([group, send(group, to_x)], axis=0)
    group = jnp.concatenate([group, send(group, to_y)], axis=0)
    outage = jnp.concatenate([group] + [send(group, to_z[k]) for k in (1, 2, 3)], axis=0)
    conts = outage.shape[0]
    own_first = (me * 2 + core) * owned
    contingency = jnp.bitwise_xor(entry_owner[:, 0] * (2 * owned) + entry_slot, own_first)

    def middle(flows_ref, out_ref, lim_ref, er_ref, ert_ref, ct_ref, ctt_ref, f_ref, limr_ref, adj_ref, every_ref):
        flows = flows_ref[...]
        hit = er_ref[...] == lax.broadcasted_iota(jnp.int32, (pairs, half), 1)
        cap = emergency * jnp.sum(jnp.where(hit, limr_ref[...], 0.0), axis=1, keepdims=True)
        cont = one_hot(ct_ref[...] == lax.broadcasted_iota(jnp.int32, (pairs, conts), 1))
        factor = f_ref[...]
        post = pick(one_hot(hit), flows) + factor * pick(cont, out_ref[...])
        adj = cont_weight * overload(post, cap)
        hot_t = one_hot(ert_ref[...] == lax.broadcasted_iota(jnp.int32, (half, pairs), 0))
        cont_t = one_hot(ctt_ref[...] == lax.broadcasted_iota(jnp.int32, (conts, pairs), 0))
        every_ref[...] = pick(cont_t, factor * adj)
        adj_ref[...] = base_weight * overload(flows, lim_ref[...]) + pick(hot_t, adj)

    adjoint, every = call(
        middle, [sds((half, scen), F32), sds((conts, scen), F32)], [VM] * 9, "penalty"
    )(
        flows, outage, limits[:, None], entry_row[:, None], entry_row[None, :],
        contingency[:, None], contingency[None, :], outage_factor[:, None], limits[None, :],
    )

    per_plane = conts // 4
    got = [send(every[k * per_plane : (k + 1) * per_plane], to_z[k]) for k in (1, 2, 3)]
    every = every[:per_plane] + got[0] + got[1] + got[2]
    for step in (lambda v: send(v, to_y), lambda v: send(v, to_x), swap):
        n = every.shape[0] // 2
        every = every[:n] + step(every[n:])

    def finish(row_ref, adj_ref, own_ref, out_ref):
        place = lax.broadcasted_iota(jnp.int32, (half, scen), 0)
        total = adj_ref[...]
        for t in range(owned):
            total = total + jnp.where(place == row_ref[t], own_ref[t : t + 1, :], 0.0)
        out_ref[...] = total.T.astype(BF16)

    adj_t = call(finish, sds((scen, half), BF16), [SM, VM, VM], "round")(outage_row, adjoint, every)
    other_t = swap(adj_t)

    scal = jnp.stack([core, *[((zz ^ k) * 4 + (spot ^ l)) for k in range(4) for l in range(4)]]).astype(jnp.int32)

    def message(n):
        return sds((scen, n * width + LANES), jnp.int16)

    block = sds((scen, width), F32)

    def backward(wanted, name, shapes, store):
        def body(scal_ref, f_ref, a_ref, b_ref, *refs):
            outs, adj = refs[:-1], refs[-1]
            adj[:, pl.ds(pl.multiple_of(scal_ref[0] * half, half), half)] = a_ref[...]
            adj[:, pl.ds(pl.multiple_of((1 - scal_ref[0]) * half, half), half)] = b_ref[...]

            def grad(k, line):
                first = pl.multiple_of(scal_ref[1 + 4 * k + line] * width, width)
                return jnp.dot(adj[...], f_ref[:, pl.ds(first, width)], preferred_element_type=F32)

            store(grad, outs)

        return call(
            body, shapes, [SM, VM, VM, VM], name, [pltpu.VMEM((scen, rows), BF16)],
            flops=2 * rows * wanted * width * scen, nbytes=wanted * width * rows * 2,
        )(scal, factors, adj_t, other_t)

    def store_1(grad, outs):
        put_coded(outs[0], [grad(3, 3), grad(3, 1)])
        put_coded(outs[1], [grad(2, 3), grad(2, 2)])

    x1, y1 = backward(4, "backward_first", [message(2), message(2)], store_1)
    x1, y1 = send(x1, to_x), send(y1, to_y)

    def store_2(grad, outs):
        put_coded(outs[0], [grad(1, 3), grad(1, 1)])
        put_coded(outs[1], [grad(0, 3), grad(0, 2)])
        for ref, (k, line) in zip(outs[2:], ((2, 1), (3, 2), (0, 1), (1, 2), (0, 0), (1, 0), (2, 0), (3, 0))):
            ref[...] = grad(k, line)

    x2b, y2b, p2x, p3y, p0x, p1y, p0, p1, p2, p3 = backward(
        12, "backward_rest", [message(2), message(2)] + [block] * 8, store_2
    )

    def add(name, *terms_of):
        flat, plan = [], []
        for terms in terms_of:
            plan.append([])
            for t in terms:
                array, which = t if isinstance(t, tuple) else (t, None)
                plan[-1].append((len(flat), which))
                flat.append(array)

        def body(*refs):
            ins, outs = refs[: len(flat)], refs[len(flat) :]
            for out, terms in zip(outs, plan):
                total = None
                for place, which in terms:
                    v = ins[place][...] if which is None else get_coded(ins[place], which, width)
                    total = v if total is None else total + v
                put_coded(out, [total])

        return call(body, [message(1)] * len(plan), [VM] * len(flat), name)(*flat)

    x2a, y2a = add("sum_2", [p2x, (y1, 0)], [p3y, (x1, 0)])
    x2a, y2a = send(x2a, to_x), send(y2a, to_y)
    x2b, y2b = send(x2b, to_x), send(y2b, to_y)
    z2, z3 = add("sum_z", [p2, (y1, 1), (x2a, 0)], [p3, (x1, 1), (y2a, 0)])
    z3, z2 = send(z3, to_z[3]), send(z2, to_z[2])
    x3, y3 = add("sum_3", [p0x, (y2b, 0)], [p1y, (x2b, 0)])
    x3, y3 = send(x3, to_x), send(y3, to_y)
    (z1,) = add("sum_z1", [p1, (x2b, 1), (y3, 0)])
    z1 = send(z1, to_z[1])

    def last(p_ref, y2b_ref, x3_ref, z1_ref, z2_ref, z3_ref, out_ref):
        total = p_ref[...] + get_coded(y2b_ref, 1, width)
        for ref in (x3_ref, z2_ref, z3_ref, z1_ref):
            total = total + get_coded(ref, 0, width)
        out_ref[...] = total.T

    return call(last, sds((width, scen), F32), [VM] * 6, "gradient")(p0, y2b, x3, z1, z2, z3)


def on_device(
    shift_factors, injections, limits, entry_row, entry_owner, entry_slot, outage_factor, outage_row
):
    rows_group, bus_cols = shift_factors.shape
    br_count = lax.axis_size("br")
    bus_count = lax.axis_size("bus")
    rows_dev = rows_group // bus_count
    owned_conts = outage_row.shape[0]
    group_conts = owned_conts * bus_count
    factor_cols = shift_factors
    partial_flows = jnp.dot(
        factor_cols,
        lax.all_gather(injections, "br", axis=0, tiled=True),
        preferred_element_type=jnp.float32,
    )
    flows = lax.psum_scatter(partial_flows, "bus", scatter_dimension=0, tiled=True)
    limit_col = limits[:, None]
    base_adj = base_weight * (
        jnp.maximum(flows - limit_col, 0.0) + jnp.minimum(flows + limit_col, 0.0)
    )
    own_outage = jnp.take(flows, outage_row, axis=0)
    owner_ids = entry_owner[:, 0]
    all_outage = lax.all_gather(own_outage, ("br", "bus"), axis=0, tiled=True)
    contingency = owner_ids * group_conts + entry_slot
    fetched = jnp.take(all_outage, contingency, axis=0)
    post_flow = jnp.take(flows, entry_row, axis=0) + outage_factor[:, None] * fetched
    emerg_cap = emergency * jnp.take(limits, entry_row)[:, None]
    entry_adj = cont_weight * (
        jnp.maximum(post_flow - emerg_cap, 0.0) + jnp.minimum(post_flow + emerg_cap, 0.0)
    )
    weighted = outage_factor[:, None] * entry_adj
    local_rows = jnp.arange(rows_dev, dtype=jnp.int32)
    row_hot = (entry_row[:, None] == local_rows[None, :]).astype(jnp.float32)
    monitored_adj = lax.dot_general(
        row_hot,
        entry_adj,
        (((0,), (0,)), ((), ())),
        precision=lax.Precision.HIGHEST,
        preferred_element_type=jnp.float32,
    )
    every_part = jax.ops.segment_sum(
        weighted, contingency, num_segments=owned_conts * br_count * bus_count
    )
    owned_adj = lax.psum_scatter(every_part, ("br", "bus"), scatter_dimension=0, tiled=True)
    outage_hot = (outage_row[:, None] == local_rows[None, :]).astype(jnp.float32)
    outage_adj = lax.dot_general(
        outage_hot,
        owned_adj,
        (((0,), (0,)), ((), ())),
        precision=lax.Precision.HIGHEST,
        preferred_element_type=jnp.float32,
    )
    adjoint = (base_adj + monitored_adj + outage_adj).astype(jnp.bfloat16)
    group_adjoint = lax.all_gather(adjoint, "bus", axis=0, tiled=True)
    return lax.psum_scatter(
        lax.dot_general(
            factor_cols, group_adjoint, (((0,), (0,)), ((), ())), preferred_element_type=jnp.float32
        ),
        "br",
        scatter_dimension=0,
        tiled=True,
    )


def solution(mesh):
    in_specs = (
        P("br", "bus"),
        P(("bus", "br"), None),
        P(("br", "bus")),
        P(("br", "bus")),
        P(("br", "bus"), None),
        P(("br", "bus")),
        P(("br", "bus")),
        P(("br", "bus")),
    )
    out_specs = P(("bus", "br"), None)
    local = on_slice if (mesh.shape["br"], mesh.shape["bus"]) == (16, 2) else on_device
    return jax.shard_map(local, mesh=mesh, in_specs=in_specs, out_specs=out_specs, check_vma=False)
```

```python
import functools

import jax
import jax.numpy as jnp
from jax import lax
from jax.experimental import pallas as pl
from jax.experimental.pallas import tpu as pltpu
from jax.sharding import PartitionSpec as P

base_weight = 1.0
cont_weight = 0.25
emergency = 1.25

F32 = jnp.float32
BF16 = jnp.bfloat16
VM = pl.BlockSpec(memory_space=pltpu.VMEM)
SM = pl.BlockSpec(memory_space=pltpu.SMEM)
LEVELS = 32000.0
LANES = 128


def call(body, out_shape, in_specs, name, scratch=(), us=0.5, limit=24):
    many = isinstance(out_shape, (tuple, list))
    return pl.pallas_call(
        body,
        out_shape=out_shape,
        in_specs=in_specs,
        out_specs=[VM] * len(out_shape) if many else VM,
        scratch_shapes=list(scratch),
        compiler_params=pltpu.CompilerParams(vmem_limit_bytes=limit << 20),
        cost_estimate=pl.CostEstimate(flops=int(us * 1.15e9), bytes_accessed=1, transcendentals=0),
        name=name,
    )


def sds(shape, dtype):
    return jax.ShapeDtypeStruct(shape, dtype)


def scaled(blocks):
    top = functools.reduce(
        jnp.maximum, [jnp.max(jnp.abs(b), axis=1, keepdims=True) for b in blocks]
    )
    power = jnp.ceil(jnp.log2(jnp.maximum(top, 1e-30)))
    return power, jnp.exp2(-power) * LEVELS


def whole(x):
    return x.astype(jnp.int32).astype(jnp.int16)


def put_coded(ref, blocks, fine=None):
    width = blocks[0].shape[1]
    power, scale = scaled(blocks)
    for n, b in enumerate(blocks):
        ref[:, n * width : (n + 1) * width] = whole(jnp.round(b * scale))
    power = jnp.broadcast_to(power, (ref.shape[0], LANES))
    if fine is not None:
        end = len(blocks) * width
        fine_power, scale = scaled([fine])
        scaled_fine = fine * scale
        high = jnp.round(scaled_fine)
        ref[:, end : end + LANES] = whole(high)
        ref[:, end + LANES : end + 2 * LANES] = whole(jnp.round((scaled_fine - high) * (2 * LEVELS)))
        lane = lax.broadcasted_iota(jnp.int32, power.shape, 1)
        power = jnp.where(lane < LANES // 2, power, fine_power)
    ref[:, ref.shape[1] - LANES :] = whole(power)


def number(x):
    return x.astype(jnp.int32).astype(F32)


def get_coded(ref, n, width):
    power = number(ref[:, ref.shape[1] - LANES :])[:, :1]
    return number(ref[:, n * width : (n + 1) * width]) * (jnp.exp2(power) * (1.0 / LEVELS))


def get_fine(ref):
    end = ref.shape[1] - 3 * LANES
    power = number(ref[:, ref.shape[1] - LANES :])[:, LANES // 2 : LANES // 2 + 1]
    value = number(ref[:, end : end + LANES]) + number(ref[:, end + LANES : end + 2 * LANES]) * (0.5 / LEVELS)
    return value * (jnp.exp2(power) * (1.0 / LEVELS))


def three(x):
    high = x.astype(BF16)
    rest = x - high.astype(F32)
    middle = rest.astype(BF16)
    low = (rest - middle.astype(F32)).astype(BF16)
    return jnp.concatenate([high, middle, low], axis=1)


def pick(hot, x):
    n = x.shape[1]
    y = jnp.dot(hot, three(x), preferred_element_type=F32)
    return y[:, :n] + y[:, n : 2 * n] + y[:, 2 * n :]


def one_hot(hit):
    return jnp.where(hit, 1.0, 0.0).astype(BF16)


def overload(x, cap):
    return jnp.maximum(x - cap, 0.0) + jnp.minimum(x + cap, 0.0)


HB = pl.BlockSpec(memory_space=pl.ANY)
DMA = pltpu.SemaphoreType.DMA


def tie(value, *others):
    return lax.optimization_barrier((value, *others))[0]


def columns(f_ref, buf, sem, scal_ref, firsts, width):
    copies = []
    for g, place in enumerate(firsts):
        start = pl.multiple_of(scal_ref[place] * width, width)
        copies.append(pltpu.make_async_copy(f_ref.at[:, pl.ds(start, width)], buf.at[g], sem.at[g]))
        copies[-1].start()
    return copies


def forward(factors, shards, blocks, total, name, core=None, us=1.0):
    rows = factors.shape[0]
    width, scen = factors.shape[1] // (4 * 4), shards[0].shape[1]
    n, half = len(blocks), rows // 2
    keep = total is not None
    spots = [(i, r) for i, v in enumerate(shards) for r in range(0, v.shape[0], width)]
    scal = jnp.stack([*blocks, 0 if core is None else core]).astype(jnp.int32)

    def body(scal_ref, f_ref, *refs):
        ins, refs = refs[: len(shards)], refs[len(shards) :]
        tot_ref, refs = (refs[0], refs[1:]) if keep else (None, refs)
        outs, (buf, acc, sem) = refs[:-3], refs[-3:]
        copies = columns(f_ref, buf, sem, scal_ref, range(n), width)
        dst = outs[0] if core is None else acc
        for g in range(n):
            copies[g].wait()
            i, r = spots[g]
            part = jnp.dot(buf[g], ins[i][r : r + width, :], preferred_element_type=F32)
            if g:
                dst[...] += part
            else:
                dst[...] = part + tot_ref[...] if keep else part
        if core is not None:
            outs[0][...] = acc[pl.ds(pl.multiple_of(scal_ref[n] * half, half), half), :]
            outs[1][...] = acc[pl.ds(pl.multiple_of((1 - scal_ref[n]) * half, half), half), :]

    ops = [scal, factors, *shards] + ([total] if keep else [])
    return call(
        body,
        sds((rows, scen), F32) if core is None else [sds((half, scen), F32)] * 2,
        [SM, HB] + [VM] * (len(ops) - 2),
        name,
        [pltpu.VMEM((n, rows, width), BF16), pltpu.VMEM((rows if core is not None else 8, scen), F32), DMA((n,))],
        us=us,
    )(*ops)


def on_slice(
    shift_factors, injections, limits, entry_row, entry_owner, entry_slot, outage_factor, outage_row
):
    rows, cols = shift_factors.shape
    width, scen = injections.shape
    half = rows // 2
    pairs = entry_row.shape[0]
    owned = outage_row.shape[0]
    group = 2 * owned
    line_conts = 4 * group
    conts = 4 * line_conts
    plane = 4 * width
    me = lax.axis_index("br")
    core = lax.axis_index("bus")
    zz, spot = me // 4, me % 4
    first = 1 + core
    second = 2 - core

    chips = [(z, s) for z in range(4) for s in range(4)]
    both = ("br", "bus")

    def to(dz, ds):
        return [(z * 4 + s, (z ^ dz) * 4 + (s ^ ds)) for z, s in chips]

    def split(ds):
        return [(2 * a + c, 2 * b + c) for c in range(2) for a, b in to(0, ds[c])]

    def send(v, dz=0, ds=0):
        return lax.ppermute(v, "br", to(dz, ds))

    def swap(v):
        return lax.ppermute(v, "bus", [(0, 1), (1, 0)])

    def send_first(v):
        return lax.ppermute(v, both, split((1, 2)))

    def send_second(v):
        return lax.ppermute(v, both, split((2, 1)))

    factors = pltpu.with_memory_space_constraint(shift_factors, pltpu.HBM)

    planes = {0: injections}
    planes[1] = send(injections, 1)
    shards = {}

    def spread(k, *after):
        a = send_first(planes[k])
        shards[k] = [planes[k], a, send_second(tie(jnp.concatenate([planes[k], a], axis=0), *after))]

    spread(0)

    def block(k, line):
        return (zz ^ k) * 4 + (spot ^ line)

    lines = [0, first, second, 3]

    other_row = swap(outage_row)
    ext = plane + LANES

    def take_rows(scal_ref, own_ref, other_ref, f_ref, *refs):
        outs, (buf, picked, sem) = refs[:4], refs[4:]
        mine = 1 - scal_ref[1]
        numbers = [own_ref[t] * mine + other_ref[t] * (1 - mine) for t in range(owned)]
        numbers += [own_ref[t] * (1 - mine) + other_ref[t] * mine + half for t in range(owned)]
        copies = []
        for c in range(group):
            start = pl.multiple_of((numbers[c] // 16) * 16, 16)
            copies.append(
                pltpu.make_async_copy(f_ref.at[pl.ds(start, 16), :], buf.at[pl.ds(16 * c, 16), :], sem.at[c])
            )
            copies[-1].start()
        lane = lax.broadcasted_iota(jnp.int32, (group, LANES), 1)
        line = lax.broadcasted_iota(jnp.int32, (group, LANES), 0)
        mark = jnp.zeros((group, LANES), F32)
        hot = jnp.zeros((group, LANES), F32)
        for c in range(group):
            high, low = numbers[c] // 16, numbers[c] % 16
            hot = hot + jnp.where((line == c) & (lane == 16 * c + low), 1.0, 0.0)
            mark = mark + jnp.where((line == c) & (lane == 0), high.astype(F32), 0.0)
            mark = mark + jnp.where((line == c) & (lane == 1), low.astype(F32), 0.0)
        for copy in copies:
            copy.wait()
        picked[...] = jnp.dot(hot.astype(BF16), buf[...], preferred_element_type=F32)
        for k in range(4):
            start = pl.multiple_of((scal_ref[0] ^ k) * plane, plane)
            outs[k][:, :plane] = picked[:, pl.ds(start, plane)].astype(BF16)
            outs[k][:, plane:] = mark.astype(BF16)

    taken = call(
        take_rows, [sds((group, ext), BF16)] * 4, [SM, SM, SM, HB], "outage_rows",
        [pltpu.VMEM((group * 16, cols), BF16), pltpu.VMEM((group, cols), F32), DMA((group,))], us=3,
    )(jnp.stack([zz, core]).astype(jnp.int32), outage_row, other_row, factors)
    planes[1] = tie(planes[1], taken[0])
    taken = [taken[0]] + [send(taken[k], k) for k in (1, 2, 3)]
    for k in (3, 2):
        planes[k] = send(tie(injections, taken[0]), k)
    spread(1)
    spread(3)

    part = forward(factors, shards[0], [block(0, line) for line in lines], None, "forward_own", us=3.5)
    planes[2] = tie(planes[2], part)
    spread(2)

    scal = jnp.stack([zz, *[spot ^ line for line in lines]]).astype(jnp.int32)

    def outage_part(scal_ref, *refs):
        rows_in, (own, one, two), (so_ref, po_ref, stack, inj) = refs[:4], refs[4:7], refs[7:]
        ins = [own[...], one[...], two[:width, :], two[width:, :]]
        for k in range(4):
            stack[pl.ds(pl.multiple_of((scal_ref[0] ^ k) * group, group), group), :] = rows_in[k][...].astype(F32)
            inj[pl.ds(pl.multiple_of(scal_ref[1 + k] * width, width), width), :] = ins[k]
        so = stack[...].astype(BF16)
        so_ref[...] = so
        po_ref[...] = jnp.dot(so[:, :plane], inj[...], preferred_element_type=F32)

    out_factors, outage = call(
        outage_part, [sds((line_conts, ext), BF16), sds((line_conts, scen), F32)], [SM] + [VM] * 7, "outage_flows",
        [pltpu.VMEM((line_conts, ext), F32), pltpu.VMEM((plane, scen), BF16)],
    )(tie(scal, part), *taken, *shards[0])
    outage = outage + send(outage, 1)
    outage = outage + send(outage, 2)
    part = forward(factors, shards[1], [block(1, line) for line in lines], part, "forward_pair", us=3.5)
    outage = tie(outage, part)
    outage = outage + swap(outage)
    outage = jnp.concatenate([outage, send(outage, 0, 1)], axis=0)
    part = forward(factors, shards[2][:2], [block(2, line) for line in lines[:2]], part, "forward_2a", us=2.9)
    outage = tie(outage, part)
    outage = jnp.concatenate([outage, send(outage, 0, 2)], axis=0)
    owner = entry_owner[:, 0]
    contingency = jnp.bitwise_xor(owner % 4, spot) * line_conts + (owner // 4) * group + entry_slot

    part = forward(factors, shards[3], [block(3, line) for line in lines], part, "forward_3", us=4)
    mine, theirs = forward(factors, shards[2][2:], [block(2, line) for line in lines[2:]], part, "forward_2b", core, us=2.9)
    theirs = swap(theirs)

    scal = jnp.concatenate([jnp.stack([zz * group + core * owned]), outage_row]).astype(jnp.int32)

    def middle(scal_ref, mine_ref, theirs_ref, out_ref, lim_ref, er_ref, ert_ref, ct_ref, ctt_ref, f_ref, limr_ref,
               adj_ref, every_t_ref, every_ref, total):
        flows = mine_ref[...] + theirs_ref[...]
        hit = er_ref[...] == lax.broadcasted_iota(jnp.int32, (pairs, half), 1)
        cap = emergency * jnp.sum(jnp.where(hit, limr_ref[...], 0.0), axis=1, keepdims=True)
        cont = one_hot(ct_ref[...] == lax.broadcasted_iota(jnp.int32, (pairs, conts), 1))
        factor = f_ref[...]
        post = pick(one_hot(hit), flows) + factor * pick(cont, out_ref[...])
        adj = cont_weight * overload(post, cap)
        hot_t = one_hot(ert_ref[...] == lax.broadcasted_iota(jnp.int32, (half, pairs), 0))
        cont_t = one_hot(ctt_ref[...] == lax.broadcasted_iota(jnp.int32, (conts, pairs), 0))
        every_ref[...] = pick(cont_t, factor * adj)
        summed = base_weight * overload(flows, lim_ref[...]) + pick(hot_t, adj)
        total[...] = summed
        place = lax.broadcasted_iota(jnp.int32, (half, scen), 0)
        out = place < 0
        for t in range(owned):
            r = scal_ref[1 + t]
            fresh = 1.0
            for u in range(t):
                fresh = fresh * jnp.where(scal_ref[1 + u] == r, 0.0, 1.0)
            own = pl.ds(scal_ref[0] + t, 1)
            every_ref[own, :] = every_ref[own, :] + fresh * total[pl.ds(r, 1), :]
            out = out | (place == r)
        adj_ref[...] = jnp.where(out, 0.0, summed).T.astype(BF16)
        every_t_ref[...] = every_ref[...].T

    adj_t, every = call(
        middle, [sds((scen, half), BF16), sds((scen, conts), F32)], [SM] + [VM] * 10, "penalty",
        [pltpu.VMEM((conts, scen), F32), pltpu.VMEM((half, scen), F32)],
    )(
        scal, mine, theirs, outage, limits[:, None], entry_row[:, None], entry_row[None, :],
        contingency[:, None], contingency[None, :], outage_factor[:, None], limits[None, :],
    )
    other_t = swap(adj_t)

    def message(n, fine=False):
        return sds((scen, n * width + (3 if fine else 1) * LANES), jnp.int16)

    grad_block = sds((scen, width), F32)

    def backward(name, adj, messages, plain, us=3.0, fine=None):
        wanted = [b for m in messages for b in m] + plain
        n = len(wanted)
        scal = jnp.stack([core, *[block(k, line) for k, line in wanted]]).astype(jnp.int32)

        def body(scal_ref, f_ref, a_ref, b_ref, *refs):
            outs, (buf, adj, sem) = refs[:-3], refs[-3:]
            more, outs = (outs[0][...], outs[1:]) if fine is not None else (None, outs)
            copies = columns(f_ref, buf, sem, scal_ref, range(1, n + 1), width)
            adj[:, pl.ds(pl.multiple_of(scal_ref[0] * half, half), half)] = a_ref[...]
            adj[:, pl.ds(pl.multiple_of((1 - scal_ref[0]) * half, half), half)] = b_ref[...]

            def grad(g):
                copies[g].wait()
                return jnp.dot(adj[...], buf[g], preferred_element_type=F32)

            g = 0
            for ref, m in zip(outs, messages):
                put_coded(ref, [grad(g + i) for i in range(len(m))], more)
                g += len(m)
            for ref in outs[len(messages) :]:
                ref[...] = grad(g)
                g += 1

        return call(
            body, [message(len(m), fine is not None) for m in messages] + [grad_block] * len(plain),
            [SM, HB] + [VM] * (2 if fine is None else 3), name,
            [pltpu.VMEM((n, rows, width), BF16), pltpu.VMEM((scen, rows), BF16), DMA((n,))],
            us=us,
        )(scal, factors, *adj, *([] if fine is None else [fine]))

    def add(name, *terms):
        flat = [t[0] if isinstance(t, tuple) else t for t in terms]

        def body(*refs):
            total = None
            for t, ref in zip(terms, refs):
                v = get_coded(ref, t[1], width) if isinstance(t, tuple) else ref[...]
                total = v if total is None else total + v
            put_coded(refs[-1], [total])

        return call(body, message(1), [VM] * len(flat), name, us=0.01)(*flat)

    def shifted(v, core_ref, on_0, on_1):
        return jnp.where(
            jnp.full(v.shape, core_ref[0]) == 0,
            pltpu.roll(v, LANES - on_0 * line_conts, 1),
            pltpu.roll(v, LANES - on_1 * line_conts, 1),
        )

    def sum_3(core_ref, p_ref, a_ref, e_ref, b_ref, t_ref):
        t_ref[...] = e_ref[...] + shifted(get_fine(a_ref), core_ref, 1, 2)
        put_coded(b_ref, [p_ref[...] + get_coded(a_ref, 0, width)], t_ref[...])

    def sum_z3(core_ref, p_ref, a_ref, b_ref, t_ref, z_ref, e_ref):
        e_ref[...] = (t_ref[...] + shifted(get_fine(b_ref), core_ref, 2, 1)).T[:line_conts, :]
        put_coded(z_ref, [p_ref[...] + get_coded(a_ref, 1, width) + get_coded(b_ref, 0, width)])

    core_1 = core[None].astype(jnp.int32)
    adj = (adj_t, other_t)
    (a3,) = backward("backward_3a", adj, [[(3, 3), (3, first)]], [], us=2.6, fine=every)
    a3_got = send_first(a3)
    adj = (tie(adj_t, a3), other_t)
    a2, p3s, p3 = backward("backward_3b", adj, [[(2, 3), (2, first)]], [(3, second), (3, 0)], us=3.3)
    a2_got = send_first(a2)
    b3, every = call(
        sum_3, [message(1, True), sds((scen, conts), F32)], [SM] + [VM] * 3, "sum_3", us=0.3
    )(core_1, tie(p3s, a2), a3_got, every)
    b3_got = send_second(b3)
    adj = (tie(adj_t, b3), other_t)
    a1, p2s, p2 = backward("backward_2", adj, [[(1, 3), (1, first)]], [(2, second), (2, 0)], us=3.5)
    a1_got = send_first(a1)
    z3, every = call(
        sum_z3, [message(1), sds((line_conts, scen), F32)], [SM] + [VM] * 4, "sum_z3", us=0.3
    )(core_1, tie(p3, a1), a3_got, b3_got, every)
    every = every + send(every, 1) + send(every, 2) + send(every, 3)
    every = every + swap(every)
    z3_got = send(z3, 3)
    b2 = add("sum_2", tie(p2s, z3), (a2_got, 0))
    b2_got = send_second(b2)

    adj = (tie(adj_t, b2), other_t)
    p1s, p1, p0d, p0f, p0s, p0 = backward("backward_0", adj, [], [(1, second), (1, 0), (0, 3), (0, first), (0, second), (0, 0)], us=0.01)
    scal = jnp.stack([spot ^ line for line in lines]).astype(jnp.int32)

    def outaged(scal_ref, e_ref, so_ref, p0_ref, ps_ref, pd_ref, pf_ref, a_ref, s_ref, o_ref, whole):
        marks = so_ref[:, plane:].astype(F32)
        number = marks[:, :1] * 16.0 + marks[:, 1:2]
        wide = jnp.broadcast_to(number, (line_conts, LANES))
        across = jnp.concatenate([wide] * (LANES // line_conts), axis=0).T[:line_conts, :line_conts]
        one = lax.broadcasted_iota(jnp.int32, (line_conts, line_conts), 0)
        two = lax.broadcasted_iota(jnp.int32, (line_conts, line_conts), 1)
        same = (one // group == two // group) & (wide[:, :line_conts] == across)
        earlier = jnp.sum(jnp.where(same & (two < one), 1.0, 0.0), axis=1, keepdims=True)
        merged = pick(one_hot(same), e_ref[...])
        final = jnp.where(earlier > 0.0, 0.0, merged).astype(BF16)
        whole[...] = lax.dot_general(final, so_ref[:, :plane], (((0,), (0,)), ((), ())), preferred_element_type=F32)

        def of(g):
            return whole[:, pl.ds(pl.multiple_of(scal_ref[g] * width, width), width)]

        put_coded(a_ref, [pd_ref[...] + of(3), pf_ref[...] + of(1)])
        s_ref[...] = ps_ref[...] + of(2)
        o_ref[...] = p0_ref[...] + of(0)

    a0, p0s, p0 = call(
        outaged, [message(2), grad_block, grad_block], [SM] + [VM] * 6, "outaged_rows", [pltpu.VMEM((scen, plane), F32)], us=0.01
    )(scal, every, out_factors, p0, p0s, p0d, p0f)
    a0_got = send_first(a0)
    z2 = add("sum_z2", tie(p2, a0), (a2_got, 1), (b2_got, 0))
    z2_got = send(z2, 2)
    b1 = add("sum_1", tie(p1s, z2), (a1_got, 0))
    b1_got = send_second(b1)

    def gather(p_ref, z3_ref, out_ref):
        out_ref[...] = p_ref[...] + get_coded(z3_ref, 0, width)

    p0 = call(gather, grad_block, [VM] * 2, "gradient_z", us=12)(tie(p0, b1), z3_got)
    b0 = add("sum_0", tie(p0s, b1, p0), (a0_got, 0))
    b0_got = send_second(b0)
    z1 = add("sum_z1", tie(p1, b0), (a1_got, 1), (b1_got, 0))
    z1_got = send(z1, 1)

    def last(p_ref, a_ref, b_ref, z1_ref, z2_ref, out_ref):
        total = p_ref[...] + get_coded(a_ref, 1, width)
        for ref in (b_ref, z2_ref, z1_ref):
            total = total + get_coded(ref, 0, width)
        out_ref[...] = total.T

    return call(last, sds((width, scen), F32), [VM] * 5, "gradient")(p0, a0_got, b0_got, z1_got, z2_got)


def on_device(
    shift_factors, injections, limits, entry_row, entry_owner, entry_slot, outage_factor, outage_row
):
    rows_group, bus_cols = shift_factors.shape
    br_count = lax.axis_size("br")
    bus_count = lax.axis_size("bus")
    rows_dev = rows_group // bus_count
    owned_conts = outage_row.shape[0]
    group_conts = owned_conts * bus_count
    factor_cols = shift_factors
    partial_flows = jnp.dot(
        factor_cols,
        lax.all_gather(injections, "br", axis=0, tiled=True),
        preferred_element_type=jnp.float32,
    )
    flows = lax.psum_scatter(partial_flows, "bus", scatter_dimension=0, tiled=True)
    limit_col = limits[:, None]
    base_adj = base_weight * (
        jnp.maximum(flows - limit_col, 0.0) + jnp.minimum(flows + limit_col, 0.0)
    )
    own_outage = jnp.take(flows, outage_row, axis=0)
    owner_ids = entry_owner[:, 0]
    all_outage = lax.all_gather(own_outage, ("br", "bus"), axis=0, tiled=True)
    contingency = owner_ids * group_conts + entry_slot
    fetched = jnp.take(all_outage, contingency, axis=0)
    post_flow = jnp.take(flows, entry_row, axis=0) + outage_factor[:, None] * fetched
    emerg_cap = emergency * jnp.take(limits, entry_row)[:, None]
    entry_adj = cont_weight * (
        jnp.maximum(post_flow - emerg_cap, 0.0) + jnp.minimum(post_flow + emerg_cap, 0.0)
    )
    weighted = outage_factor[:, None] * entry_adj
    local_rows = jnp.arange(rows_dev, dtype=jnp.int32)
    row_hot = (entry_row[:, None] == local_rows[None, :]).astype(jnp.float32)
    monitored_adj = lax.dot_general(
        row_hot,
        entry_adj,
        (((0,), (0,)), ((), ())),
        precision=lax.Precision.HIGHEST,
        preferred_element_type=jnp.float32,
    )
    every_part = jax.ops.segment_sum(
        weighted, contingency, num_segments=owned_conts * br_count * bus_count
    )
    owned_adj = lax.psum_scatter(every_part, ("br", "bus"), scatter_dimension=0, tiled=True)
    outage_hot = (outage_row[:, None] == local_rows[None, :]).astype(jnp.float32)
    outage_adj = lax.dot_general(
        outage_hot,
        owned_adj,
        (((0,), (0,)), ((), ())),
        precision=lax.Precision.HIGHEST,
        preferred_element_type=jnp.float32,
    )
    adjoint = (base_adj + monitored_adj + outage_adj).astype(jnp.bfloat16)
    group_adjoint = lax.all_gather(adjoint, "bus", axis=0, tiled=True)
    return lax.psum_scatter(
        lax.dot_general(
            factor_cols, group_adjoint, (((0,), (0,)), ((), ())), preferred_element_type=jnp.float32
        ),
        "br",
        scatter_dimension=0,
        tiled=True,
    )


def solution(mesh):
    in_specs = (
        P("br", "bus"),
        P(("bus", "br"), None),
        P(("br", "bus")),
        P(("br", "bus")),
        P(("br", "bus"), None),
        P(("br", "bus")),
        P(("br", "bus")),
        P(("br", "bus")),
    )
    out_specs = P(("bus", "br"), None)
    local = on_slice if (mesh.shape["br"], mesh.shape["bus"]) == (16, 2) else on_device
    return jax.shard_map(local, mesh=mesh, in_specs=in_specs, out_specs=out_specs, check_vma=False)
```

```python
import functools

import jax
import jax.numpy as jnp
from jax import lax
from jax.experimental import pallas as pl
from jax.experimental.pallas import tpu as pltpu
from jax.sharding import PartitionSpec as P

base_weight = 1.0
cont_weight = 0.25
emergency = 1.25

F32 = jnp.float32
BF16 = jnp.bfloat16
VM = pl.BlockSpec(memory_space=pltpu.VMEM)
SM = pl.BlockSpec(memory_space=pltpu.SMEM)
LEVELS = 32000.0
LANES = 128


def call(body, out_shape, in_specs, name, scratch=(), us=0.5, limit=24):
    many = isinstance(out_shape, (tuple, list))
    return pl.pallas_call(
        body,
        out_shape=out_shape,
        in_specs=in_specs,
        out_specs=[VM] * len(out_shape) if many else VM,
        scratch_shapes=list(scratch),
        compiler_params=pltpu.CompilerParams(vmem_limit_bytes=limit << 20),
        cost_estimate=pl.CostEstimate(flops=int(us * 1.15e9), bytes_accessed=1, transcendentals=0),
        name=name,
    )


def sds(shape, dtype):
    return jax.ShapeDtypeStruct(shape, dtype)


def scaled(blocks):
    top = functools.reduce(
        jnp.maximum, [jnp.max(jnp.abs(b), axis=1, keepdims=True) for b in blocks]
    )
    power = jnp.ceil(jnp.log2(jnp.maximum(top, 1e-30)))
    return power, jnp.exp2(-power) * LEVELS


def whole(x):
    return x.astype(jnp.int32).astype(jnp.int16)


def put_coded(ref, blocks, fine=None):
    width = blocks[0].shape[1]
    power, scale = scaled(blocks)
    for n, b in enumerate(blocks):
        ref[:, n * width : (n + 1) * width] = whole(jnp.round(b * scale))
    power = jnp.broadcast_to(power, (ref.shape[0], LANES))
    if fine is not None:
        end = len(blocks) * width
        fine_power, scale = scaled([fine])
        scaled_fine = fine * scale
        high = jnp.round(scaled_fine)
        ref[:, end : end + LANES] = whole(high)
        ref[:, end + LANES : end + 2 * LANES] = whole(jnp.round((scaled_fine - high) * (2 * LEVELS)))
        lane = lax.broadcasted_iota(jnp.int32, power.shape, 1)
        power = jnp.where(lane < LANES // 2, power, fine_power)
    ref[:, ref.shape[1] - LANES :] = whole(power)


def number(x):
    return x.astype(jnp.int32).astype(F32)


def get_coded(ref, n, width):
    power = number(ref[:, ref.shape[1] - LANES :])[:, :1]
    return number(ref[:, n * width : (n + 1) * width]) * (jnp.exp2(power) * (1.0 / LEVELS))


def get_fine(ref):
    end = ref.shape[1] - 3 * LANES
    power = number(ref[:, ref.shape[1] - LANES :])[:, LANES // 2 : LANES // 2 + 1]
    value = number(ref[:, end : end + LANES]) + number(ref[:, end + LANES : end + 2 * LANES]) * (0.5 / LEVELS)
    return value * (jnp.exp2(power) * (1.0 / LEVELS))


def three(x):
    high = x.astype(BF16)
    rest = x - high.astype(F32)
    middle = rest.astype(BF16)
    low = (rest - middle.astype(F32)).astype(BF16)
    return jnp.concatenate([high, middle, low], axis=1)


def pick(hot, x):
    n = x.shape[1]
    y = jnp.dot(hot, three(x), preferred_element_type=F32)
    return y[:, :n] + y[:, n : 2 * n] + y[:, 2 * n :]


def one_hot(hit):
    return jnp.where(hit, 1.0, 0.0).astype(BF16)


def overload(x, cap):
    return jnp.maximum(x - cap, 0.0) + jnp.minimum(x + cap, 0.0)


HB = pl.BlockSpec(memory_space=pl.ANY)
DMA = pltpu.SemaphoreType.DMA


def tie(value, *others):
    return lax.optimization_barrier((value, *others))[0]


def here():
    me = lax.axis_index("br")
    return me // 4, me % 4, lax.axis_index("bus")


def spot_of(line):
    _, spot, core = here()
    return spot ^ {0: 0, "a": 1 + core, "b": 2 - core, 3: 3}[line]


def at(index, size):
    return pl.ds(pl.multiple_of(index * size, size), size)


def columns(f_ref, buf, sem, wanted, width):
    copies = []
    for g, (k, line) in enumerate(wanted):
        place = (here()[0] ^ k) * 4 + spot_of(line)
        copies.append(pltpu.make_async_copy(f_ref.at[:, at(place, width)], buf.at[g], sem.at[g]))
        copies[-1].start()
    return copies


def forward(factors, shards, wanted, total, name, parted=False, us=1.0):
    rows = factors.shape[0]
    width, scen = factors.shape[1] // (4 * 4), shards[0].shape[1]
    n, half = len(wanted), rows // 2
    keep = total is not None
    spots = [(i, r) for i, v in enumerate(shards) for r in range(0, v.shape[0], width)]

    def body(f_ref, *refs):
        ins, refs = refs[: len(shards)], refs[len(shards) :]
        tot_ref, refs = (refs[0], refs[1:]) if keep else (None, refs)
        outs, (buf, acc, sem) = refs[:-3], refs[-3:]
        copies = columns(f_ref, buf, sem, wanted, width)
        dst = acc if parted else outs[0]
        for g in range(n):
            copies[g].wait()
            i, r = spots[g]
            part = jnp.dot(buf[g], ins[i][r : r + width, :], preferred_element_type=F32)
            if g:
                dst[...] += part
            else:
                dst[...] = part + tot_ref[...] if keep else part
        if parted:
            core = here()[2]
            outs[0][...] = acc[at(core, half), :]
            outs[1][...] = acc[at(1 - core, half), :]

    ops = [factors, *shards] + ([total] if keep else [])
    return call(
        body,
        [sds((half, scen), F32)] * 2 if parted else sds((rows, scen), F32),
        [HB] + [VM] * (len(ops) - 1),
        name,
        [pltpu.VMEM((n, rows, width), BF16), pltpu.VMEM((rows if parted else 8, scen), F32), DMA((n,))],
        us=us,
    )(*ops)


def on_slice(
    shift_factors, injections, limits, entry_row, entry_owner, entry_slot, outage_factor, outage_row
):
    rows, cols = shift_factors.shape
    width, scen = injections.shape
    half = rows // 2
    pairs = entry_row.shape[0]
    owned = outage_row.shape[0]
    group = 2 * owned
    line_conts = 4 * group
    conts = 4 * line_conts
    plane = 4 * width
    me = lax.axis_index("br")
    core = lax.axis_index("bus")
    zz, spot = me // 4, me % 4

    chips = [(z, s) for z in range(4) for s in range(4)]
    both = ("br", "bus")

    def to(dz, ds):
        return [(z * 4 + s, (z ^ dz) * 4 + (s ^ ds)) for z, s in chips]

    def split(ds):
        return [(2 * a + c, 2 * b + c) for c in range(2) for a, b in to(0, ds[c])]

    def send(v, dz=0, ds=0):
        return lax.ppermute(v, "br", to(dz, ds))

    def swap(v):
        return lax.ppermute(v, "bus", [(0, 1), (1, 0)])

    def send_first(v):
        return lax.ppermute(v, both, split((1, 2)))

    def send_second(v):
        return lax.ppermute(v, both, split((2, 1)))

    factors = pltpu.with_memory_space_constraint(shift_factors, pltpu.HBM)

    planes = {0: injections}
    planes[1] = send(injections, 1)
    shards = {}

    def spread(k, *after):
        a = send_first(planes[k])
        shards[k] = [planes[k], a, send_second(tie(jnp.concatenate([planes[k], a], axis=0), *after))]

    a = send_first(injections)
    shards[0] = [injections, a, send_second(injections), send_second(a)]

    lines = [0, "a", "b", 3]

    other_row = swap(outage_row)
    ext = plane + LANES

    def take_rows(own_ref, other_ref, f_ref, *refs):
        outs, (buf, picked, sem) = refs[:4], refs[4:]
        plane_at, _, core = here()
        mine = 1 - core
        numbers = [own_ref[t] * mine + other_ref[t] * (1 - mine) for t in range(owned)]
        numbers += [own_ref[t] * (1 - mine) + other_ref[t] * mine + half for t in range(owned)]
        copies = []
        for c in range(group):
            start = pl.multiple_of((numbers[c] // 16) * 16, 16)
            copies.append(
                pltpu.make_async_copy(f_ref.at[pl.ds(start, 16), :], buf.at[pl.ds(16 * c, 16), :], sem.at[c])
            )
            copies[-1].start()
        lane = lax.broadcasted_iota(jnp.int32, (group, LANES), 1)
        line = lax.broadcasted_iota(jnp.int32, (group, LANES), 0)
        mark = jnp.zeros((group, LANES), F32)
        hot = jnp.zeros((group, LANES), F32)
        for c in range(group):
            high, low = numbers[c] // 16, numbers[c] % 16
            hot = hot + jnp.where((line == c) & (lane == 16 * c + low), 1.0, 0.0)
            mark = mark + jnp.where((line == c) & (lane == 0), high.astype(F32), 0.0)
            mark = mark + jnp.where((line == c) & (lane == 1), low.astype(F32), 0.0)
        for copy in copies:
            copy.wait()
        picked[...] = jnp.dot(hot.astype(BF16), buf[...], preferred_element_type=F32)
        for k in range(4):
            outs[k][:, :plane] = picked[:, at(plane_at ^ k, plane)].astype(BF16)
            outs[k][:, plane:] = mark.astype(BF16)

    taken = call(
        take_rows, [sds((group, ext), BF16)] * 4, [SM, SM, HB], "outage_rows",
        [pltpu.VMEM((group * 16, cols), BF16), pltpu.VMEM((group, cols), F32), DMA((group,))], us=3,
    )(outage_row, other_row, factors)
    for k in (3, 2):
        planes[k] = send(tie(injections, other_row), k)
    taken = [taken[0]] + [send(taken[k], k) for k in (1, 2, 3)]

    part = forward(factors, shards[0], [(0, line) for line in lines], None, "forward_own", us=3.5)
    planes[2] = tie(planes[2], part)
    for k in (1, 3, 2):
        spread(k)

    def outage_part(*refs):
        rows_in, ins, (so_ref, po_ref, stack, inj) = refs[:4], refs[4:8], refs[8:]
        for k in range(4):
            stack[at(here()[0] ^ k, group), :] = rows_in[k][...].astype(F32)
            inj[at(spot_of(lines[k]), width), :] = ins[k][...]
        so = stack[...].astype(BF16)
        so_ref[...] = so
        po_ref[...] = jnp.dot(so[:, :plane], inj[...], preferred_element_type=F32)

    out_factors, outage = call(
        outage_part, [sds((line_conts, ext), BF16), sds((line_conts, scen), F32)], [VM] * 8, "outage_flows",
        [pltpu.VMEM((line_conts, ext), F32), pltpu.VMEM((plane, scen), BF16)],
    )(tie(taken[0], part, planes[2]), *taken[1:], *shards[0])
    outage = outage + send(outage, 1)
    outage = tie(outage, shards[1][1], shards[3][1])
    outage = outage + send(outage, 2)
    outage = tie(outage, shards[2][1], shards[1][2])
    outage = outage + swap(outage)
    summed = outage
    outage = tie(outage, shards[3][2])
    outage = jnp.concatenate([outage, send(outage, 0, 1)], axis=0)
    wanted = [(k, line) for k in (1, 3) for line in lines] + [(2, line) for line in lines[:2]]
    part = forward(tie(factors, summed), shards[1] + shards[3] + shards[2][:2], wanted, part, "forward_most", us=6)
    outage = tie(outage, part)
    outage = jnp.concatenate([outage, send(outage, 0, 2)], axis=0)
    owner = entry_owner[:, 0]
    contingency = jnp.bitwise_xor(owner % 4, spot) * line_conts + (owner // 4) * group + entry_slot

    wanted = [(2, line) for line in lines[2:]]
    mine, theirs = forward(factors, shards[2][2:], wanted, part, "forward_last", True, us=2.4)
    theirs = swap(theirs)

    def middle(row_ref, mine_ref, theirs_ref, out_ref, lim_ref, er_ref, ert_ref, ct_ref, ctt_ref, f_ref, limr_ref,
               adj_ref, every_t_ref, every_ref, total):
        flows = mine_ref[...] + theirs_ref[...]
        hit = er_ref[...] == lax.broadcasted_iota(jnp.int32, (pairs, half), 1)
        cap = emergency * jnp.sum(jnp.where(hit, limr_ref[...], 0.0), axis=1, keepdims=True)
        cont = one_hot(ct_ref[...] == lax.broadcasted_iota(jnp.int32, (pairs, conts), 1))
        factor = f_ref[...]
        post = pick(one_hot(hit), flows) + factor * pick(cont, out_ref[...])
        adj = cont_weight * overload(post, cap)
        hot_t = one_hot(ert_ref[...] == lax.broadcasted_iota(jnp.int32, (half, pairs), 0))
        cont_t = one_hot(ctt_ref[...] == lax.broadcasted_iota(jnp.int32, (conts, pairs), 0))
        every_ref[...] = pick(cont_t, factor * adj)
        summed = base_weight * overload(flows, lim_ref[...]) + pick(hot_t, adj)
        total[...] = summed
        place = lax.broadcasted_iota(jnp.int32, (half, scen), 0)
        out = place < 0
        for t in range(owned):
            r = row_ref[t]
            fresh = 1.0
            for u in range(t):
                fresh = fresh * jnp.where(row_ref[u] == r, 0.0, 1.0)
            own = pl.ds(here()[0] * group + here()[2] * owned + t, 1)
            every_ref[own, :] = every_ref[own, :] + fresh * total[pl.ds(r, 1), :]
            out = out | (place == r)
        adj_ref[...] = jnp.where(out, 0.0, summed).T.astype(BF16)
        every_t_ref[...] = every_ref[...].T

    adj_t, every = call(
        middle, [sds((scen, half), BF16), sds((scen, conts), F32)], [SM] + [VM] * 10, "penalty",
        [pltpu.VMEM((conts, scen), F32), pltpu.VMEM((half, scen), F32)],
    )(
        outage_row, mine, theirs, outage, limits[:, None], entry_row[:, None], entry_row[None, :],
        contingency[:, None], contingency[None, :], outage_factor[:, None], limits[None, :],
    )
    other_t = swap(adj_t)

    def message(n, fine=False):
        return sds((scen, n * width + (3 if fine else 1) * LANES), jnp.int16)

    grad_block = sds((scen, width), F32)

    def backward(name, adj, messages, plain, us=3.0, fine=None):
        wanted = [b for m in messages for b in m] + plain
        n = len(wanted)

        def body(f_ref, a_ref, b_ref, *refs):
            outs, (buf, adj, sem) = refs[:-3], refs[-3:]
            more, outs = (outs[0][...], outs[1:]) if fine is not None else (None, outs)
            copies = columns(f_ref, buf, sem, wanted, width)
            adj[:, at(here()[2], half)] = a_ref[...]
            adj[:, at(1 - here()[2], half)] = b_ref[...]

            def grad(g):
                copies[g].wait()
                return jnp.dot(adj[...], buf[g], preferred_element_type=F32)

            g = 0
            for ref, m in zip(outs, messages):
                put_coded(ref, [grad(g + i) for i in range(len(m))], more)
                g += len(m)
            for ref in outs[len(messages) :]:
                ref[...] = grad(g)
                g += 1

        return call(
            body, [message(len(m), fine is not None) for m in messages] + [grad_block] * len(plain),
            [HB] + [VM] * (2 if fine is None else 3), name,
            [pltpu.VMEM((n, rows, width), BF16), pltpu.VMEM((scen, rows), BF16), DMA((n,))],
            us=us,
        )(factors, *adj, *([] if fine is None else [fine]))

    def add(name, *terms):
        flat = [t[0] if isinstance(t, tuple) else t for t in terms]

        def body(*refs):
            total = None
            for t, ref in zip(terms, refs):
                v = get_coded(ref, t[1], width) if isinstance(t, tuple) else ref[...]
                total = v if total is None else total + v
            put_coded(refs[-1], [total])

        return call(body, message(1), [VM] * len(flat), name, us=0.01)(*flat)

    def shifted(v, on_0, on_1):
        return jnp.where(
            jnp.full(v.shape, here()[2]) == 0,
            pltpu.roll(v, LANES - on_0 * line_conts, 1),
            pltpu.roll(v, LANES - on_1 * line_conts, 1),
        )

    def sum_3(p_ref, a_ref, e_ref, b_ref, t_ref):
        t_ref[...] = e_ref[...] + shifted(get_fine(a_ref), 1, 2)
        put_coded(b_ref, [p_ref[...] + get_coded(a_ref, 0, width)], t_ref[...])

    def sum_z3(p_ref, a_ref, b_ref, t_ref, z_ref, e_ref):
        e_ref[...] = (t_ref[...] + shifted(get_fine(b_ref), 2, 1)).T[:line_conts, :]
        put_coded(z_ref, [p_ref[...] + get_coded(a_ref, 1, width) + get_coded(b_ref, 0, width)])

    adj = (adj_t, other_t)
    (a3,) = backward("backward_3a", adj, [[(3, 3), (3, "a")]], [], us=2.6, fine=every)
    a3_got = send_first(a3)
    adj = (tie(adj_t, a3), other_t)
    a2, p3s, p3 = backward("backward_3b", adj, [[(2, 3), (2, "a")]], [(3, "b"), (3, 0)], us=3.3)
    a2_got = send_first(a2)
    b3, every = call(
        sum_3, [message(1, True), sds((scen, conts), F32)], [VM] * 3, "sum_3", us=0.3
    )(tie(p3s, a2), a3_got, every)
    b3_got = send_second(b3)
    adj = (tie(adj_t, b3), other_t)
    wanted = [(2, "b"), (2, 0), (1, "b"), (1, 0)]
    a1, p2s, p2, p1s, p1 = backward("backward_2", adj, [[(1, 3), (1, "a")]], wanted, us=3.5)
    a1_got = send_first(a1)
    z3, every = call(
        sum_z3, [message(1), sds((line_conts, scen), F32)], [VM] * 4, "sum_z3", us=0.3
    )(tie(p3, a1), a3_got, b3_got, every)
    every = every + send(every, 1) + send(every, 2) + send(every, 3)
    every = every + swap(every)
    z3_got = send(z3, 3)
    b2 = add("sum_2", tie(p2s, z3), (a2_got, 0))
    b2_got = send_second(b2)
    b1 = add("sum_1", tie(p1s, b2), (a1_got, 0))
    b1_got = send_second(b1)


    def outaged(f_ref, a_ref, b_ref, e_ref, so_ref, out_ref, s_ref, o_ref, buf, adj, more, sem):
        copies = columns(f_ref, buf, sem, [(0, line) for line in (3, "a", "b", 0)], width)
        adj[:, at(here()[2], half)] = a_ref[...]
        adj[:, at(1 - here()[2], half)] = b_ref[...]
        marks = so_ref[:, plane:].astype(F32)
        row = marks[:, :1] * 16.0 + marks[:, 1:2]
        wide = jnp.broadcast_to(row, (line_conts, LANES))
        across = jnp.concatenate([wide] * (LANES // line_conts), axis=0).T[:line_conts, :line_conts]
        one = lax.broadcasted_iota(jnp.int32, (line_conts, line_conts), 0)
        two = lax.broadcasted_iota(jnp.int32, (line_conts, line_conts), 1)
        same = (one // group == two // group) & (wide[:, :line_conts] == across)
        earlier = jnp.sum(jnp.where(same & (two < one), 1.0, 0.0), axis=1, keepdims=True)
        merged = pick(one_hot(same), e_ref[...])
        final = jnp.where(earlier > 0.0, 0.0, merged).astype(BF16)
        more[...] = lax.dot_general(final, so_ref[:, :plane], (((0,), (0,)), ((), ())), preferred_element_type=F32)

        def grad(g, line):
            copies[g].wait()
            return jnp.dot(adj[...], buf[g], preferred_element_type=F32) + more[:, at(spot_of(line), width)]

        put_coded(out_ref, [grad(0, 3), grad(1, "a")])
        s_ref[...] = grad(2, "b")
        o_ref[...] = grad(3, 0)

    a0, p0s, p0 = call(
        outaged, [message(2), grad_block, grad_block], [HB] + [VM] * 4, "backward_0",
        [pltpu.VMEM((4, rows, width), BF16), pltpu.VMEM((scen, rows), BF16), pltpu.VMEM((scen, plane), F32), DMA((4,))],
        us=0.01,
    )(factors, tie(adj_t, b1), other_t, every, out_factors)
    a0_got = send_first(a0)
    def gather(p_ref, z3_ref, out_ref):
        out_ref[...] = p_ref[...] + get_coded(z3_ref, 0, width)

    p0 = call(gather, grad_block, [VM] * 2, "gradient_z", us=12)(tie(p0, a0), z3_got)
    z2 = add("sum_z2", tie(p2, p0), (a2_got, 1), (b2_got, 0))
    z2_got = send(z2, 2)
    z1 = add("sum_z1", tie(p1, z2), (a1_got, 1), (b1_got, 0))
    z1_got = send(z1, 1)

    b0 = add("sum_0", tie(p0s, z1), (a0_got, 0))
    b0_got = send_second(b0)
    def last(p_ref, a_ref, b_ref, z1_ref, z2_ref, out_ref):
        total = p_ref[...] + get_coded(a_ref, 1, width)
        for ref in (b_ref, z2_ref, z1_ref):
            total = total + get_coded(ref, 0, width)
        out_ref[...] = total.T

    return call(last, sds((width, scen), F32), [VM] * 5, "gradient")(p0, a0_got, b0_got, z1_got, z2_got)


def on_device(
    shift_factors, injections, limits, entry_row, entry_owner, entry_slot, outage_factor, outage_row
):
    rows_group, bus_cols = shift_factors.shape
    br_count = lax.axis_size("br")
    bus_count = lax.axis_size("bus")
    rows_dev = rows_group // bus_count
    owned_conts = outage_row.shape[0]
    group_conts = owned_conts * bus_count
    factor_cols = shift_factors
    partial_flows = jnp.dot(
        factor_cols,
        lax.all_gather(injections, "br", axis=0, tiled=True),
        preferred_element_type=jnp.float32,
    )
    flows = lax.psum_scatter(partial_flows, "bus", scatter_dimension=0, tiled=True)
    limit_col = limits[:, None]
    base_adj = base_weight * (
        jnp.maximum(flows - limit_col, 0.0) + jnp.minimum(flows + limit_col, 0.0)
    )
    own_outage = jnp.take(flows, outage_row, axis=0)
    owner_ids = entry_owner[:, 0]
    all_outage = lax.all_gather(own_outage, ("br", "bus"), axis=0, tiled=True)
    contingency = owner_ids * group_conts + entry_slot
    fetched = jnp.take(all_outage, contingency, axis=0)
    post_flow = jnp.take(flows, entry_row, axis=0) + outage_factor[:, None] * fetched
    emerg_cap = emergency * jnp.take(limits, entry_row)[:, None]
    entry_adj = cont_weight * (
        jnp.maximum(post_flow - emerg_cap, 0.0) + jnp.minimum(post_flow + emerg_cap, 0.0)
    )
    weighted = outage_factor[:, None] * entry_adj
    local_rows = jnp.arange(rows_dev, dtype=jnp.int32)
    row_hot = (entry_row[:, None] == local_rows[None, :]).astype(jnp.float32)
    monitored_adj = lax.dot_general(
        row_hot,
        entry_adj,
        (((0,), (0,)), ((), ())),
        precision=lax.Precision.HIGHEST,
        preferred_element_type=jnp.float32,
    )
    every_part = jax.ops.segment_sum(
        weighted, contingency, num_segments=owned_conts * br_count * bus_count
    )
    owned_adj = lax.psum_scatter(every_part, ("br", "bus"), scatter_dimension=0, tiled=True)
    outage_hot = (outage_row[:, None] == local_rows[None, :]).astype(jnp.float32)
    outage_adj = lax.dot_general(
        outage_hot,
        owned_adj,
        (((0,), (0,)), ((), ())),
        precision=lax.Precision.HIGHEST,
        preferred_element_type=jnp.float32,
    )
    adjoint = (base_adj + monitored_adj + outage_adj).astype(jnp.bfloat16)
    group_adjoint = lax.all_gather(adjoint, "bus", axis=0, tiled=True)
    return lax.psum_scatter(
        lax.dot_general(
            factor_cols, group_adjoint, (((0,), (0,)), ((), ())), preferred_element_type=jnp.float32
        ),
        "br",
        scatter_dimension=0,
        tiled=True,
    )


def solution(mesh):
    in_specs = (
        P("br", "bus"),
        P(("bus", "br"), None),
        P(("br", "bus")),
        P(("br", "bus")),
        P(("br", "bus"), None),
        P(("br", "bus")),
        P(("br", "bus")),
        P(("br", "bus")),
    )
    out_specs = P(("bus", "br"), None)
    local = on_slice if (mesh.shape["br"], mesh.shape["bus"]) == (16, 2) else on_device
    return jax.shard_map(local, mesh=mesh, in_specs=in_specs, out_specs=out_specs, check_vma=False)
```

```python
import functools

import jax
import jax.numpy as jnp
from jax import lax
from jax.experimental import pallas as pl
from jax.experimental.pallas import tpu as pltpu
from jax.sharding import PartitionSpec as P

base_weight = 1.0
cont_weight = 0.25
emergency = 1.25

F32 = jnp.float32
BF16 = jnp.bfloat16
VM = pl.BlockSpec(memory_space=pltpu.VMEM)
SM = pl.BlockSpec(memory_space=pltpu.SMEM)
LEVELS = 32000.0
LANES = 128


def call(body, out_shape, in_specs, name, scratch=(), us=0.5, limit=24):
    many = isinstance(out_shape, (tuple, list))
    return pl.pallas_call(
        body,
        out_shape=out_shape,
        in_specs=in_specs,
        out_specs=[VM] * len(out_shape) if many else VM,
        scratch_shapes=list(scratch),
        compiler_params=pltpu.CompilerParams(vmem_limit_bytes=limit << 20),
        cost_estimate=pl.CostEstimate(flops=int(us * 1.15e9), bytes_accessed=1, transcendentals=0),
        name=name,
    )


def sds(shape, dtype):
    return jax.ShapeDtypeStruct(shape, dtype)


def scaled(blocks):
    top = functools.reduce(
        jnp.maximum, [jnp.max(jnp.abs(b), axis=1, keepdims=True) for b in blocks]
    )
    power = jnp.ceil(jnp.log2(jnp.maximum(top, 1e-30)))
    return power, jnp.exp2(-power) * LEVELS


def whole(x):
    return x.astype(jnp.int32).astype(jnp.int16)


def put_coded(ref, blocks, fine=None):
    width = blocks[0].shape[1]
    power, scale = scaled(blocks)
    for n, b in enumerate(blocks):
        ref[:, n * width : (n + 1) * width] = whole(jnp.round(b * scale))
    power = jnp.broadcast_to(power, (ref.shape[0], LANES))
    if fine is not None:
        end = len(blocks) * width
        fine_power, scale = scaled([fine])
        scaled_fine = fine * scale
        high = jnp.round(scaled_fine)
        ref[:, end : end + LANES] = whole(high)
        ref[:, end + LANES : end + 2 * LANES] = whole(jnp.round((scaled_fine - high) * (2 * LEVELS)))
        lane = lax.broadcasted_iota(jnp.int32, power.shape, 1)
        power = jnp.where(lane < LANES // 2, power, fine_power)
    ref[:, ref.shape[1] - LANES :] = whole(power)


def number(x):
    return x.astype(jnp.int32).astype(F32)


def get_coded(ref, n, width):
    power = number(ref[:, ref.shape[1] - LANES :])[:, :1]
    return number(ref[:, n * width : (n + 1) * width]) * (jnp.exp2(power) * (1.0 / LEVELS))


def get_fine(ref):
    end = ref.shape[1] - 3 * LANES
    power = number(ref[:, ref.shape[1] - LANES :])[:, LANES // 2 : LANES // 2 + 1]
    value = number(ref[:, end : end + LANES]) + number(ref[:, end + LANES : end + 2 * LANES]) * (0.5 / LEVELS)
    return value * (jnp.exp2(power) * (1.0 / LEVELS))


def three(x):
    high = x.astype(BF16)
    rest = x - high.astype(F32)
    middle = rest.astype(BF16)
    low = (rest - middle.astype(F32)).astype(BF16)
    return jnp.concatenate([high, middle, low], axis=1)


def pick(hot, x):
    n = x.shape[1]
    y = jnp.dot(hot, three(x), preferred_element_type=F32)
    return y[:, :n] + y[:, n : 2 * n] + y[:, 2 * n :]


def one_hot(hit):
    return jnp.where(hit, 1.0, 0.0).astype(BF16)


def overload(x, cap):
    return jnp.maximum(x - cap, 0.0) + jnp.minimum(x + cap, 0.0)


HB = pl.BlockSpec(memory_space=pl.ANY)
DMA = pltpu.SemaphoreType.DMA


def tie(value, *others):
    return lax.optimization_barrier((value, *others))[0]


def here():
    me = lax.axis_index("br")
    return me // 4, me % 4, lax.axis_index("bus")


def spot_of(line):
    _, spot, core = here()
    return spot ^ {0: 0, "a": 1 + core, "b": 2 - core, 3: 3}[line]


def at(index, size):
    return pl.ds(pl.multiple_of(index * size, size), size)


def columns(f_ref, buf, sem, wanted, width):
    copies = []
    for g, (k, line) in enumerate(wanted):
        place = (here()[0] ^ k) * 4 + spot_of(line)
        into = buf[g] if isinstance(buf, (tuple, list)) else buf.at[g]
        copies.append(pltpu.make_async_copy(f_ref.at[:, at(place, width)], into, sem.at[g]))
        copies[-1].start()
    return copies


def forward(factors, shards, wanted, total, name, parted=False, us=1.0, ready=(), ahead=()):
    rows = factors.shape[0]
    width, scen = factors.shape[1] // (4 * 4), shards[0].shape[1]
    n, half = len(wanted), rows // 2
    keep = total is not None
    spots = [(i, r) for i, v in enumerate(shards) for r in range(0, v.shape[0], width)]

    def body(f_ref, *refs):
        ins, refs = refs[: len(shards)], refs[len(shards) :]
        tot_ref, refs = (refs[0], refs[1:]) if keep else (None, refs)
        blocks, refs = refs[: len(ready)], refs[len(ready) :]
        outs, (buf, acc, sem, later) = refs[:-4], refs[-4:]
        copies = [] if ready else columns(f_ref, buf, sem, wanted, width)
        extra = columns(f_ref, outs[len(outs) - len(ahead) :], later, ahead, width)
        dst = acc if parted else outs[0]
        for g in range(n):
            if copies:
                copies[g].wait()
            i, r = spots[g]
            part = jnp.dot(blocks[g][...] if ready else buf[g], ins[i][r : r + width, :], preferred_element_type=F32)
            if g:
                dst[...] += part
            else:
                dst[...] = part + tot_ref[...] if keep else part
        if parted:
            core = here()[2]
            outs[0][...] = acc[at(core, half), :]
            outs[1][...] = acc[at(1 - core, half), :]
        for copy in extra:
            copy.wait()

    ops = [factors, *shards] + ([total] if keep else []) + list(ready)
    shapes = [sds((half, scen), F32)] * 2 if parted else [sds((rows, scen), F32)]
    shapes += [sds((rows, width), BF16)] * len(ahead)
    return call(
        body,
        shapes if len(shapes) > 1 else shapes[0],
        [HB] + [VM] * (len(ops) - 1),
        name,
        [pltpu.VMEM((1 if ready else n, rows, width), BF16), pltpu.VMEM((rows if parted else 8, scen), F32), DMA((n,)),
         DMA((max(1, len(ahead)),))],
        us=us,
    )(*ops)


def on_slice(
    shift_factors, injections, limits, entry_row, entry_owner, entry_slot, outage_factor, outage_row
):
    rows, cols = shift_factors.shape
    width, scen = injections.shape
    half = rows // 2
    pairs = entry_row.shape[0]
    owned = outage_row.shape[0]
    group = 2 * owned
    line_conts = 4 * group
    conts = 4 * line_conts
    plane = 4 * width
    me = lax.axis_index("br")
    core = lax.axis_index("bus")
    zz, spot = me // 4, me % 4

    chips = [(z, s) for z in range(4) for s in range(4)]
    both = ("br", "bus")

    def to(dz, ds):
        return [(z * 4 + s, (z ^ dz) * 4 + (s ^ ds)) for z, s in chips]

    def split(ds):
        return [(2 * a + c, 2 * b + c) for c in range(2) for a, b in to(0, ds[c])]

    def send(v, dz=0, ds=0):
        return lax.ppermute(v, "br", to(dz, ds))

    def swap(v):
        return lax.ppermute(v, "bus", [(0, 1), (1, 0)])

    def send_first(v):
        return lax.ppermute(v, both, split((1, 2)))

    def send_second(v):
        return lax.ppermute(v, both, split((2, 1)))

    factors = pltpu.with_memory_space_constraint(shift_factors, pltpu.HBM)

    planes = {0: injections}
    planes[1] = send(injections, 1)
    shards = {}

    def spread(k, *after):
        a = send_first(planes[k])
        shards[k] = [planes[k], a, send_second(tie(jnp.concatenate([planes[k], a], axis=0), *after))]

    a = send_first(injections)
    shards[0] = [injections, a, send_second(injections), send_second(a)]

    lines = [0, "a", "b", 3]

    other_row = swap(outage_row)
    ext = plane + LANES

    def take_rows(own_ref, other_ref, f_ref, *refs):
        outs, (buf, picked, sem) = refs[:4], refs[4:]
        plane_at, _, core = here()
        mine = 1 - core
        numbers = [own_ref[t] * mine + other_ref[t] * (1 - mine) for t in range(owned)]
        numbers += [own_ref[t] * (1 - mine) + other_ref[t] * mine + half for t in range(owned)]
        copies = []
        for c in range(group):
            start = pl.multiple_of((numbers[c] // 16) * 16, 16)
            copies.append(
                pltpu.make_async_copy(f_ref.at[pl.ds(start, 16), :], buf.at[pl.ds(16 * c, 16), :], sem.at[c])
            )
            copies[-1].start()
        lane = lax.broadcasted_iota(jnp.int32, (group, LANES), 1)
        line = lax.broadcasted_iota(jnp.int32, (group, LANES), 0)
        mark = jnp.zeros((group, LANES), F32)
        hot = jnp.zeros((group, LANES), F32)
        for c in range(group):
            high, low = numbers[c] // 16, numbers[c] % 16
            hot = hot + jnp.where((line == c) & (lane == 16 * c + low), 1.0, 0.0)
            mark = mark + jnp.where((line == c) & (lane == 0), high.astype(F32), 0.0)
            mark = mark + jnp.where((line == c) & (lane == 1), low.astype(F32), 0.0)
        for copy in copies:
            copy.wait()
        picked[...] = jnp.dot(hot.astype(BF16), buf[...], preferred_element_type=F32)
        for k in range(4):
            outs[k][:, :plane] = picked[:, at(plane_at ^ k, plane)].astype(BF16)
            outs[k][:, plane:] = mark.astype(BF16)

    taken = call(
        take_rows, [sds((group, ext), BF16)] * 4, [SM, SM, HB], "outage_rows",
        [pltpu.VMEM((group * 16, cols), BF16), pltpu.VMEM((group, cols), F32), DMA((group,))], us=3,
    )(outage_row, other_row, factors)
    for k in (3, 2):
        planes[k] = send(tie(injections, other_row), k)
    taken = [taken[0]] + [send(taken[k], k) for k in (1, 2, 3)]

    part = forward(factors, shards[0], [(0, line) for line in lines], None, "forward_own", us=3.5)
    planes[2] = tie(planes[2], part)
    for k in (1, 3, 2):
        spread(k)

    def outage_part(*refs):
        rows_in, ins, (so_ref, po_ref, stack, inj) = refs[:4], refs[4:8], refs[8:]
        for k in range(4):
            stack[at(here()[0] ^ k, group), :] = rows_in[k][...].astype(F32)
            inj[at(spot_of(lines[k]), width), :] = ins[k][...]
        so = stack[...].astype(BF16)
        so_ref[...] = so
        po_ref[...] = jnp.dot(so[:, :plane], inj[...], preferred_element_type=F32)

    out_factors, outage = call(
        outage_part, [sds((line_conts, ext), BF16), sds((line_conts, scen), F32)], [VM] * 8, "outage_flows",
        [pltpu.VMEM((line_conts, ext), F32), pltpu.VMEM((plane, scen), BF16)],
    )(tie(taken[0], part, planes[2]), *taken[1:], *shards[0])
    outage = outage + send(outage, 1)
    outage = tie(outage, shards[1][1], shards[3][1])
    outage = outage + send(outage, 2)
    outage = tie(outage, shards[2][1], shards[1][2])
    summed = outage
    outage = outage + swap(outage)
    outage = tie(outage, shards[3][2])
    outage = jnp.concatenate([outage, send(outage, 0, 1)], axis=0)
    wanted = [(k, line) for k in (1, 3) for line in lines] + [(2, line) for line in lines[:2]]
    part = forward(tie(factors, summed), shards[1] + shards[3] + shards[2][:2], wanted, part, "forward_most", us=6)
    outage = tie(outage, part)
    outage = jnp.concatenate([outage, send(outage, 0, 2)], axis=0)
    owner = entry_owner[:, 0]
    contingency = jnp.bitwise_xor(owner % 4, spot) * line_conts + (owner // 4) * group + entry_slot

    wanted = [(2, line) for line in lines[2:]]
    mine, theirs, *ready = forward(
        factors, shards[2][2:], wanted, part, "forward_last", True, us=2.4, ahead=[(3, 3), (3, "a")]
    )
    theirs = swap(theirs)

    def middle(row_ref, mine_ref, theirs_ref, out_ref, lim_ref, er_ref, ert_ref, ct_ref, ctt_ref, f_ref, limr_ref,
               adj_ref, every_t_ref, every_ref, total):
        flows = mine_ref[...] + theirs_ref[...]
        hit = er_ref[...] == lax.broadcasted_iota(jnp.int32, (pairs, half), 1)
        cap = emergency * jnp.sum(jnp.where(hit, limr_ref[...], 0.0), axis=1, keepdims=True)
        cont = one_hot(ct_ref[...] == lax.broadcasted_iota(jnp.int32, (pairs, conts), 1))
        factor = f_ref[...]
        post = pick(one_hot(hit), flows) + factor * pick(cont, out_ref[...])
        adj = cont_weight * overload(post, cap)
        hot_t = one_hot(ert_ref[...] == lax.broadcasted_iota(jnp.int32, (half, pairs), 0))
        cont_t = one_hot(ctt_ref[...] == lax.broadcasted_iota(jnp.int32, (conts, pairs), 0))
        every_ref[...] = pick(cont_t, factor * adj)
        summed = base_weight * overload(flows, lim_ref[...]) + pick(hot_t, adj)
        total[...] = summed
        place = lax.broadcasted_iota(jnp.int32, (half, scen), 0)
        out = place < 0
        for t in range(owned):
            r = row_ref[t]
            fresh = 1.0
            for u in range(t):
                fresh = fresh * jnp.where(row_ref[u] == r, 0.0, 1.0)
            own = pl.ds(here()[0] * group + here()[2] * owned + t, 1)
            every_ref[own, :] = every_ref[own, :] + fresh * total[pl.ds(r, 1), :]
            out = out | (place == r)
        adj_ref[...] = jnp.where(out, 0.0, summed).T.astype(BF16)
        every_t_ref[...] = every_ref[...].T

    adj_t, every = call(
        middle, [sds((scen, half), BF16), sds((scen, conts), F32)], [SM] + [VM] * 10, "penalty",
        [pltpu.VMEM((conts, scen), F32), pltpu.VMEM((half, scen), F32)],
    )(
        outage_row, mine, theirs, outage, limits[:, None], entry_row[:, None], entry_row[None, :],
        contingency[:, None], contingency[None, :], outage_factor[:, None], limits[None, :],
    )
    other_t = swap(adj_t)

    def message(n, fine=False):
        return sds((scen, n * width + (3 if fine else 1) * LANES), jnp.int16)

    grad_block = sds((scen, width), F32)

    def backward(name, adj, messages, plain, us=3.0, fine=None, ready=()):
        wanted = [b for m in messages for b in m] + plain
        n = len(wanted)

        def body(f_ref, a_ref, b_ref, *refs):
            outs, (buf, adj, sem) = refs[:-3], refs[-3:]
            more, outs = (outs[0][...], outs[1:]) if fine is not None else (None, outs)
            blocks, outs = outs[: len(ready)], outs[len(ready) :]
            copies = [] if ready else columns(f_ref, buf, sem, wanted, width)
            adj[:, at(here()[2], half)] = a_ref[...]
            adj[:, at(1 - here()[2], half)] = b_ref[...]

            def grad(g):
                if copies:
                    copies[g].wait()
                return jnp.dot(adj[...], blocks[g][...] if ready else buf[g], preferred_element_type=F32)

            g = 0
            for ref, m in zip(outs, messages):
                put_coded(ref, [grad(g + i) for i in range(len(m))], more)
                g += len(m)
            for ref in outs[len(messages) :]:
                ref[...] = grad(g)
                g += 1

        return call(
            body, [message(len(m), fine is not None) for m in messages] + [grad_block] * len(plain),
            [HB] + [VM] * ((2 if fine is None else 3) + len(ready)), name,
            [pltpu.VMEM((1 if ready else n, rows, width), BF16), pltpu.VMEM((scen, rows), BF16), DMA((n,))],
            us=us,
        )(factors, *adj, *([] if fine is None else [fine]), *ready)

    def add(name, *terms):
        flat = [t[0] if isinstance(t, tuple) else t for t in terms]

        def body(*refs):
            total = None
            for t, ref in zip(terms, refs):
                v = get_coded(ref, t[1], width) if isinstance(t, tuple) else ref[...]
                total = v if total is None else total + v
            put_coded(refs[-1], [total])

        return call(body, message(1), [VM] * len(flat), name, us=0.01)(*flat)

    def shifted(v, on_0, on_1):
        return jnp.where(
            jnp.full(v.shape, here()[2]) == 0,
            pltpu.roll(v, LANES - on_0 * line_conts, 1),
            pltpu.roll(v, LANES - on_1 * line_conts, 1),
        )

    def sum_3(p_ref, a_ref, e_ref, b_ref, t_ref):
        t_ref[...] = e_ref[...] + shifted(get_fine(a_ref), 1, 2)
        put_coded(b_ref, [p_ref[...] + get_coded(a_ref, 0, width)], t_ref[...])

    def sum_z3(p_ref, a_ref, b_ref, t_ref, z_ref, e_ref):
        e_ref[...] = (t_ref[...] + shifted(get_fine(b_ref), 2, 1)).T[:line_conts, :]
        put_coded(z_ref, [p_ref[...] + get_coded(a_ref, 1, width) + get_coded(b_ref, 0, width)])

    adj = (adj_t, other_t)
    (a3,) = backward("backward_3a", adj, [[(3, 3), (3, "a")]], [], us=1.5, fine=every, ready=ready)
    a3_got = send_first(a3)
    adj = (tie(adj_t, a3), other_t)
    a2, p3s, p3 = backward("backward_3b", adj, [[(2, 3), (2, "a")]], [(3, "b"), (3, 0)], us=3.3)
    a2_got = send_first(a2)
    adj = (tie(adj_t, a2), other_t)
    wanted = [(2, "b"), (2, 0), (1, "b"), (1, 0)]
    a1, p2s, p2, p1s, p1 = backward("backward_2", adj, [[(1, 3), (1, "a")]], wanted, us=3.5)
    b3, every = call(
        sum_3, [message(1, True), sds((scen, conts), F32)], [VM] * 3, "sum_3", us=0.3
    )(tie(p3s, a1), a3_got, every)
    b3_got = send_second(b3)
    adj = (tie(adj_t, b3), other_t)
    p0d, p0f, p0s, p0 = backward("backward_0", adj, [], [(0, 3), (0, "a"), (0, "b"), (0, 0)], us=3)
    z3, every = call(
        sum_z3, [message(1), sds((line_conts, scen), F32)], [VM] * 4, "sum_z3", us=0.3
    )(tie(p3, p0), a3_got, b3_got, every)
    every = every + send(every, 1) + send(every, 2) + send(every, 3)
    every = every + swap(every)
    a1_got = send_first(tie(a1, z3))
    z3_got = send(z3, 3)
    b2 = add("sum_2", tie(p2s, z3), (a2_got, 0))
    b2_got = send_second(b2)
    b1 = add("sum_1", tie(p1s, b2), (a1_got, 0))
    b1_got = send_second(b1)


    def outaged(d_ref, f_ref, p_ref, q_ref, e_ref, so_ref, out_ref, s_ref, o_ref, more):
        marks = so_ref[:, plane:].astype(F32)
        row = marks[:, :1] * 16.0 + marks[:, 1:2]
        wide = jnp.broadcast_to(row, (line_conts, LANES))
        across = jnp.concatenate([wide] * (LANES // line_conts), axis=0).T[:line_conts, :line_conts]
        one = lax.broadcasted_iota(jnp.int32, (line_conts, line_conts), 0)
        two = lax.broadcasted_iota(jnp.int32, (line_conts, line_conts), 1)
        same = (one // group == two // group) & (wide[:, :line_conts] == across)
        earlier = jnp.sum(jnp.where(same & (two < one), 1.0, 0.0), axis=1, keepdims=True)
        merged = pick(one_hot(same), e_ref[...])
        final = jnp.where(earlier > 0.0, 0.0, merged).astype(BF16)
        more[...] = lax.dot_general(final, so_ref[:, :plane], (((0,), (0,)), ((), ())), preferred_element_type=F32)

        def grad(ref, line):
            return ref[...] + more[:, at(spot_of(line), width)]

        put_coded(out_ref, [grad(d_ref, 3), grad(f_ref, "a")])
        s_ref[...] = grad(p_ref, "b")
        o_ref[...] = grad(q_ref, 0)

    a0, p0s, p0 = call(
        outaged, [message(2), grad_block, grad_block], [VM] * 6, "outaged_rows", [pltpu.VMEM((scen, plane), F32)], us=0.01
    )(tie(p0d, b1), p0f, p0s, p0, every, out_factors)
    a0_got = send_first(a0)

    def gather(p_ref, z3_ref, out_ref):
        out_ref[...] = p_ref[...] + get_coded(z3_ref, 0, width)

    p0 = call(gather, grad_block, [VM] * 2, "gradient_z", us=12)(tie(p0, a0), z3_got)
    z2 = add("sum_z2", tie(p2, a0), (a2_got, 1), (b2_got, 0))
    z2_got = send(z2, 2)
    z1 = add("sum_z1", tie(p1, z2, p0), (a1_got, 1), (b1_got, 0))
    z1_got = send(z1, 1)

    b0 = add("sum_0", tie(p0s, z1), (a0_got, 0))
    b0_got = send_second(b0)
    def last(p_ref, a_ref, b_ref, z1_ref, z2_ref, out_ref):
        total = p_ref[...] + get_coded(a_ref, 1, width)
        for ref in (b_ref, z2_ref, z1_ref):
            total = total + get_coded(ref, 0, width)
        out_ref[...] = total.T

    return call(last, sds((width, scen), F32), [VM] * 5, "gradient")(p0, a0_got, b0_got, z1_got, z2_got)


def on_device(
    shift_factors, injections, limits, entry_row, entry_owner, entry_slot, outage_factor, outage_row
):
    rows_group, bus_cols = shift_factors.shape
    br_count = lax.axis_size("br")
    bus_count = lax.axis_size("bus")
    rows_dev = rows_group // bus_count
    owned_conts = outage_row.shape[0]
    group_conts = owned_conts * bus_count
    factor_cols = shift_factors
    partial_flows = jnp.dot(
        factor_cols,
        lax.all_gather(injections, "br", axis=0, tiled=True),
        preferred_element_type=jnp.float32,
    )
    flows = lax.psum_scatter(partial_flows, "bus", scatter_dimension=0, tiled=True)
    limit_col = limits[:, None]
    base_adj = base_weight * (
        jnp.maximum(flows - limit_col, 0.0) + jnp.minimum(flows + limit_col, 0.0)
    )
    own_outage = jnp.take(flows, outage_row, axis=0)
    owner_ids = entry_owner[:, 0]
    all_outage = lax.all_gather(own_outage, ("br", "bus"), axis=0, tiled=True)
    contingency = owner_ids * group_conts + entry_slot
    fetched = jnp.take(all_outage, contingency, axis=0)
    post_flow = jnp.take(flows, entry_row, axis=0) + outage_factor[:, None] * fetched
    emerg_cap = emergency * jnp.take(limits, entry_row)[:, None]
    entry_adj = cont_weight * (
        jnp.maximum(post_flow - emerg_cap, 0.0) + jnp.minimum(post_flow + emerg_cap, 0.0)
    )
    weighted = outage_factor[:, None] * entry_adj
    local_rows = jnp.arange(rows_dev, dtype=jnp.int32)
    row_hot = (entry_row[:, None] == local_rows[None, :]).astype(jnp.float32)
    monitored_adj = lax.dot_general(
        row_hot,
        entry_adj,
        (((0,), (0,)), ((), ())),
        precision=lax.Precision.HIGHEST,
        preferred_element_type=jnp.float32,
    )
    every_part = jax.ops.segment_sum(
        weighted, contingency, num_segments=owned_conts * br_count * bus_count
    )
    owned_adj = lax.psum_scatter(every_part, ("br", "bus"), scatter_dimension=0, tiled=True)
    outage_hot = (outage_row[:, None] == local_rows[None, :]).astype(jnp.float32)
    outage_adj = lax.dot_general(
        outage_hot,
        owned_adj,
        (((0,), (0,)), ((), ())),
        precision=lax.Precision.HIGHEST,
        preferred_element_type=jnp.float32,
    )
    adjoint = (base_adj + monitored_adj + outage_adj).astype(jnp.bfloat16)
    group_adjoint = lax.all_gather(adjoint, "bus", axis=0, tiled=True)
    return lax.psum_scatter(
        lax.dot_general(
            factor_cols, group_adjoint, (((0,), (0,)), ((), ())), preferred_element_type=jnp.float32
        ),
        "br",
        scatter_dimension=0,
        tiled=True,
    )


def solution(mesh):
    in_specs = (
        P("br", "bus"),
        P(("bus", "br"), None),
        P(("br", "bus")),
        P(("br", "bus")),
        P(("br", "bus"), None),
        P(("br", "bus")),
        P(("br", "bus")),
        P(("br", "bus")),
    )
    out_specs = P(("bus", "br"), None)
    local = on_slice if (mesh.shape["br"], mesh.shape["bus"]) == (16, 2) else on_device
    return jax.shard_map(local, mesh=mesh, in_specs=in_specs, out_specs=out_specs, check_vma=False)
```

```python
import functools

import jax
import jax.numpy as jnp
from jax import lax
from jax.experimental import pallas as pl
from jax.experimental.pallas import tpu as pltpu
from jax.sharding import PartitionSpec as P

base_weight = 1.0
cont_weight = 0.25
emergency = 1.25

F32 = jnp.float32
BF16 = jnp.bfloat16
VM = pl.BlockSpec(memory_space=pltpu.VMEM)
SM = pl.BlockSpec(memory_space=pltpu.SMEM)
LEVELS = 32000.0
LANES = 128


def call(body, out_shape, in_specs, name, scratch=(), us=0.5, limit=16):
    many = isinstance(out_shape, (tuple, list))
    return pl.pallas_call(
        body,
        out_shape=out_shape,
        in_specs=in_specs,
        out_specs=[VM] * len(out_shape) if many else VM,
        scratch_shapes=list(scratch),
        compiler_params=pltpu.CompilerParams(vmem_limit_bytes=limit << 20),
        cost_estimate=pl.CostEstimate(flops=int(us * 1.15e9), bytes_accessed=1, transcendentals=0),
        name=name,
    )


def sds(shape, dtype):
    return jax.ShapeDtypeStruct(shape, dtype)


def scaled(blocks):
    top = functools.reduce(
        jnp.maximum, [jnp.max(jnp.abs(b), axis=1, keepdims=True) for b in blocks]
    )
    power = jnp.ceil(jnp.log2(jnp.maximum(top, 1e-30)))
    return power, jnp.exp2(-power) * LEVELS


def whole(x):
    return x.astype(jnp.int32).astype(jnp.int16)


def put_coded(ref, blocks, fine=None):
    width = blocks[0].shape[1]
    power, scale = scaled(blocks)
    for n, b in enumerate(blocks):
        ref[:, n * width : (n + 1) * width] = whole(jnp.round(b * scale))
    power = jnp.broadcast_to(power, (ref.shape[0], LANES))
    if fine is not None:
        end = len(blocks) * width
        fine_power, scale = scaled([fine])
        scaled_fine = fine * scale
        high = jnp.round(scaled_fine)
        ref[:, end : end + LANES] = whole(high)
        ref[:, end + LANES : end + 2 * LANES] = whole(jnp.round((scaled_fine - high) * (2 * LEVELS)))
        lane = lax.broadcasted_iota(jnp.int32, power.shape, 1)
        power = jnp.where(lane < LANES // 2, power, fine_power)
    ref[:, ref.shape[1] - LANES :] = whole(power)


def number(x):
    return x.astype(jnp.int32).astype(F32)


def get_coded(ref, n, width):
    power = number(ref[:, ref.shape[1] - LANES :])[:, :1]
    return number(ref[:, n * width : (n + 1) * width]) * (jnp.exp2(power) * (1.0 / LEVELS))


def get_fine(ref):
    end = ref.shape[1] - 3 * LANES
    power = number(ref[:, ref.shape[1] - LANES :])[:, LANES // 2 : LANES // 2 + 1]
    value = number(ref[:, end : end + LANES]) + number(ref[:, end + LANES : end + 2 * LANES]) * (0.5 / LEVELS)
    return value * (jnp.exp2(power) * (1.0 / LEVELS))


def three(x):
    high = x.astype(BF16)
    rest = x - high.astype(F32)
    middle = rest.astype(BF16)
    low = (rest - middle.astype(F32)).astype(BF16)
    return jnp.concatenate([high, middle, low], axis=1)


def pick(hot, x):
    n = x.shape[1]
    y = jnp.dot(hot, three(x), preferred_element_type=F32)
    return y[:, :n] + y[:, n : 2 * n] + y[:, 2 * n :]


def one_hot(hit):
    return jnp.where(hit, 1.0, 0.0).astype(BF16)


def overload(x, cap):
    return jnp.maximum(x - cap, 0.0) + jnp.minimum(x + cap, 0.0)


HB = pl.BlockSpec(memory_space=pl.ANY)
DMA = pltpu.SemaphoreType.DMA


def tie(value, *others):
    return lax.optimization_barrier((value, *others))[0]


def here():
    me = lax.axis_index("br")
    return me // 4, me % 4, lax.axis_index("bus")


def spot_of(line):
    _, spot, core = here()
    return spot ^ {0: 0, "a": 1 + core, "b": 2 - core, 3: 3}[line]


def at(index, size):
    return pl.ds(pl.multiple_of(index * size, size), size)


def columns(f_ref, buf, sem, wanted, width):
    copies = []
    for g, (k, line) in enumerate(wanted):
        place = (here()[0] ^ k) * 4 + spot_of(line)
        into = buf[g] if isinstance(buf, (tuple, list)) else buf.at[g]
        copies.append(pltpu.make_async_copy(f_ref.at[:, at(place, width)], into, sem.at[g]))
        copies[-1].start()
    return copies


def forward(factors, shards, wanted, total, name, parted=False, us=1.0, ready=(), ahead=()):
    rows = factors.shape[0]
    width, scen = factors.shape[1] // (4 * 4), shards[0].shape[1]
    n, half = len(wanted), rows // 2
    keep = total is not None
    spots = [(i, r) for i, v in enumerate(shards) for r in range(0, v.shape[0], width)]

    def body(f_ref, *refs):
        ins, refs = refs[: len(shards)], refs[len(shards) :]
        tot_ref, refs = (refs[0], refs[1:]) if keep else (None, refs)
        blocks, refs = refs[: len(ready)], refs[len(ready) :]
        outs, (buf, acc, sem, later) = refs[:-4], refs[-4:]
        copies = [] if ready else columns(f_ref, buf, sem, wanted, width)
        extra = columns(f_ref, outs[len(outs) - len(ahead) :], later, ahead, width)
        dst = acc if parted else outs[0]
        for g in range(n):
            if copies:
                copies[g].wait()
            i, r = spots[g]
            part = jnp.dot(blocks[g][...] if ready else buf[g], ins[i][r : r + width, :], preferred_element_type=F32)
            if g:
                dst[...] += part
            else:
                dst[...] = part + tot_ref[...] if keep else part
        if parted:
            core = here()[2]
            outs[0][...] = acc[at(core, half), :]
            outs[1][...] = acc[at(1 - core, half), :]
        for copy in extra:
            copy.wait()

    ops = [factors, *shards] + ([total] if keep else []) + list(ready)
    shapes = [sds((half, scen), F32)] * 2 if parted else [sds((rows, scen), F32)]
    shapes += [sds((rows, width), BF16)] * len(ahead)
    return call(
        body,
        shapes if len(shapes) > 1 else shapes[0],
        [HB] + [VM] * (len(ops) - 1),
        name,
        [pltpu.VMEM((1 if ready else n, rows, width), BF16), pltpu.VMEM((rows if parted else 8, scen), F32), DMA((n,)),
         DMA((max(1, len(ahead)),))],
        us=us,
    )(*ops)


def on_slice(
    shift_factors, injections, limits, entry_row, entry_owner, entry_slot, outage_factor, outage_row
):
    rows, cols = shift_factors.shape
    width, scen = injections.shape
    half = rows // 2
    pairs = entry_row.shape[0]
    owned = outage_row.shape[0]
    group = 2 * owned
    line_conts = 4 * group
    conts = 4 * line_conts
    plane = 4 * width
    me = lax.axis_index("br")
    core = lax.axis_index("bus")
    zz, spot = me // 4, me % 4

    chips = [(z, s) for z in range(4) for s in range(4)]
    both = ("br", "bus")

    def to(dz, ds):
        return [(z * 4 + s, (z ^ dz) * 4 + (s ^ ds)) for z, s in chips]

    def split(ds):
        return [(2 * a + c, 2 * b + c) for c in range(2) for a, b in to(0, ds[c])]

    def send(v, dz=0, ds=0):
        return lax.ppermute(v, "br", to(dz, ds))

    def swap(v):
        return lax.ppermute(v, "bus", [(0, 1), (1, 0)])

    def send_first(v):
        return lax.ppermute(v, both, split((1, 2)))

    def send_second(v):
        return lax.ppermute(v, both, split((2, 1)))

    factors = pltpu.with_memory_space_constraint(shift_factors, pltpu.HBM)

    planes = {0: injections}
    planes[1] = send(injections, 1)
    shards = {}

    def spread(k, *after):
        a = send_first(planes[k])
        shards[k] = [planes[k], a, send_second(tie(jnp.concatenate([planes[k], a], axis=0), *after))]

    a = send_first(injections)
    shards[0] = [injections, a, send_second(injections), send_second(a)]

    lines = [0, "a", "b", 3]

    other_row = swap(outage_row)
    ext = plane + LANES

    def take_rows(own_ref, other_ref, f_ref, *refs):
        outs, (buf, picked, sem) = refs[:4], refs[4:]
        plane_at, _, core = here()
        mine = 1 - core
        numbers = [own_ref[t] * mine + other_ref[t] * (1 - mine) for t in range(owned)]
        numbers += [own_ref[t] * (1 - mine) + other_ref[t] * mine + half for t in range(owned)]
        copies = []
        for c in range(group):
            start = pl.multiple_of((numbers[c] // 16) * 16, 16)
            copies.append(
                pltpu.make_async_copy(f_ref.at[pl.ds(start, 16), :], buf.at[pl.ds(16 * c, 16), :], sem.at[c])
            )
            copies[-1].start()
        lane = lax.broadcasted_iota(jnp.int32, (group, LANES), 1)
        line = lax.broadcasted_iota(jnp.int32, (group, LANES), 0)
        mark = jnp.zeros((group, LANES), F32)
        hot = jnp.zeros((group, LANES), F32)
        for c in range(group):
            high, low = numbers[c] // 16, numbers[c] % 16
            hot = hot + jnp.where((line == c) & (lane == 16 * c + low), 1.0, 0.0)
            mark = mark + jnp.where((line == c) & (lane == 0), high.astype(F32), 0.0)
            mark = mark + jnp.where((line == c) & (lane == 1), low.astype(F32), 0.0)
        for copy in copies:
            copy.wait()
        picked[...] = jnp.dot(hot.astype(BF16), buf[...], preferred_element_type=F32)
        for k in range(4):
            outs[k][:, :plane] = picked[:, at(plane_at ^ k, plane)].astype(BF16)
            outs[k][:, plane:] = mark.astype(BF16)

    taken = call(
        take_rows, [sds((group, ext), BF16)] * 4, [SM, SM, HB], "outage_rows",
        [pltpu.VMEM((group * 16, cols), BF16), pltpu.VMEM((group, cols), F32), DMA((group,))], us=3,
    )(outage_row, other_row, factors)
    for k in (3, 2):
        planes[k] = send(tie(injections, other_row), k)
    taken = [taken[0]] + [send(taken[k], k) for k in (1, 2, 3)]

    part = forward(factors, shards[0], [(0, line) for line in lines], None, "forward_own", us=3.5)
    planes[2] = tie(planes[2], part)
    for k in (1, 3, 2):
        spread(k)

    def outage_part(*refs):
        rows_in, ins, (so_ref, po_ref, stack, inj) = refs[:4], refs[4:8], refs[8:]
        for k in range(4):
            stack[at(here()[0] ^ k, group), :] = rows_in[k][...].astype(F32)
            inj[at(spot_of(lines[k]), width), :] = ins[k][...]
        so = stack[...].astype(BF16)
        so_ref[...] = so
        po_ref[...] = jnp.dot(so[:, :plane], inj[...], preferred_element_type=F32)

    out_factors, outage = call(
        outage_part, [sds((line_conts, ext), BF16), sds((line_conts, scen), F32)], [VM] * 8, "outage_flows",
        [pltpu.VMEM((line_conts, ext), F32), pltpu.VMEM((plane, scen), BF16)],
    )(tie(taken[0], part, planes[2]), *taken[1:], *shards[0])
    outage = outage + send(outage, 1)
    outage = tie(outage, shards[1][1], shards[3][1])
    outage = outage + send(outage, 2)
    outage = tie(outage, shards[2][1], shards[1][2])
    summed = outage
    outage = outage + swap(outage)
    outage = tie(outage, shards[3][2])
    outage = jnp.concatenate([outage, send(outage, 0, 1)], axis=0)
    wanted = [(k, line) for k in (1, 3) for line in lines] + [(2, line) for line in lines[:2]]
    part = forward(tie(factors, summed), shards[1] + shards[3] + shards[2][:2], wanted, part, "forward_most", us=6)
    outage = tie(outage, part)
    outage = jnp.concatenate([outage, send(outage, 0, 2)], axis=0)
    owner = entry_owner[:, 0]
    contingency = jnp.bitwise_xor(owner % 4, spot) * line_conts + (owner // 4) * group + entry_slot

    wanted = [(2, line) for line in lines[2:]]
    mine, theirs, *ready = forward(
        factors, shards[2][2:], wanted, part, "forward_last", True, us=2.4, ahead=[(3, 3), (3, "a")]
    )
    theirs = swap(theirs)

    def middle(row_ref, mine_ref, theirs_ref, out_ref, lim_ref, er_ref, ert_ref, ct_ref, ctt_ref, f_ref, limr_ref,
               adj_ref, every_t_ref, every_ref, total):
        flows = mine_ref[...] + theirs_ref[...]
        hit = er_ref[...] == lax.broadcasted_iota(jnp.int32, (pairs, half), 1)
        cap = emergency * jnp.sum(jnp.where(hit, limr_ref[...], 0.0), axis=1, keepdims=True)
        cont = one_hot(ct_ref[...] == lax.broadcasted_iota(jnp.int32, (pairs, conts), 1))
        factor = f_ref[...]
        post = pick(one_hot(hit), flows) + factor * pick(cont, out_ref[...])
        adj = cont_weight * overload(post, cap)
        hot_t = one_hot(ert_ref[...] == lax.broadcasted_iota(jnp.int32, (half, pairs), 0))
        cont_t = one_hot(ctt_ref[...] == lax.broadcasted_iota(jnp.int32, (conts, pairs), 0))
        every_ref[...] = pick(cont_t, factor * adj)
        summed = base_weight * overload(flows, lim_ref[...]) + pick(hot_t, adj)
        total[...] = summed
        place = lax.broadcasted_iota(jnp.int32, (half, scen), 0)
        out = place < 0
        for t in range(owned):
            r = row_ref[t]
            fresh = 1.0
            for u in range(t):
                fresh = fresh * jnp.where(row_ref[u] == r, 0.0, 1.0)
            own = pl.ds(here()[0] * group + here()[2] * owned + t, 1)
            every_ref[own, :] = every_ref[own, :] + fresh * total[pl.ds(r, 1), :]
            out = out | (place == r)
        adj_ref[...] = jnp.where(out, 0.0, summed).T.astype(BF16)
        every_t_ref[...] = every_ref[...].T

    adj_t, every = call(
        middle, [sds((scen, half), BF16), sds((scen, conts), F32)], [SM] + [VM] * 10, "penalty",
        [pltpu.VMEM((conts, scen), F32), pltpu.VMEM((half, scen), F32)],
    )(
        outage_row, mine, theirs, outage, limits[:, None], entry_row[:, None], entry_row[None, :],
        contingency[:, None], contingency[None, :], outage_factor[:, None], limits[None, :],
    )
    other_t = swap(adj_t)

    def message(n, fine=False):
        return sds((scen, n * width + (3 if fine else 1) * LANES), jnp.int16)

    grad_block = sds((scen, width), F32)

    def backward(name, adj, messages, plain, us=3.0, fine=None, ready=()):
        wanted = [b for m in messages for b in m] + plain
        n = len(wanted)

        def body(f_ref, a_ref, b_ref, *refs):
            outs, (buf, adj, sem) = refs[:-3], refs[-3:]
            more, outs = (outs[0][...], outs[1:]) if fine is not None else (None, outs)
            blocks, outs = outs[: len(ready)], outs[len(ready) :]
            copies = [] if ready else columns(f_ref, buf, sem, wanted, width)
            adj[:, at(here()[2], half)] = a_ref[...]
            adj[:, at(1 - here()[2], half)] = b_ref[...]

            def grad(g):
                if copies:
                    copies[g].wait()
                return jnp.dot(adj[...], blocks[g][...] if ready else buf[g], preferred_element_type=F32)

            g = 0
            for ref, m in zip(outs, messages):
                put_coded(ref, [grad(g + i) for i in range(len(m))], more)
                g += len(m)
            for ref in outs[len(messages) :]:
                ref[...] = grad(g)
                g += 1

        return call(
            body, [message(len(m), fine is not None) for m in messages] + [grad_block] * len(plain),
            [HB] + [VM] * ((2 if fine is None else 3) + len(ready)), name,
            [pltpu.VMEM((1 if ready else n, rows, width), BF16), pltpu.VMEM((scen, rows), BF16), DMA((n,))],
            us=us,
        )(factors, *adj, *([] if fine is None else [fine]), *ready)

    def add(name, *terms):
        flat = [t[0] if isinstance(t, tuple) else t for t in terms]

        def body(*refs):
            total = None
            for t, ref in zip(terms, refs):
                v = get_coded(ref, t[1], width) if isinstance(t, tuple) else ref[...]
                total = v if total is None else total + v
            put_coded(refs[-1], [total])

        return call(body, message(1), [VM] * len(flat), name, us=0.01)(*flat)

    def shifted(v, on_0, on_1):
        return jnp.where(
            jnp.full(v.shape, here()[2]) == 0,
            pltpu.roll(v, LANES - on_0 * line_conts, 1),
            pltpu.roll(v, LANES - on_1 * line_conts, 1),
        )

    def sum_3(p_ref, a_ref, e_ref, b_ref, t_ref):
        t_ref[...] = e_ref[...] + shifted(get_fine(a_ref), 1, 2)
        put_coded(b_ref, [p_ref[...] + get_coded(a_ref, 0, width)], t_ref[...])

    def sum_z3(p_ref, a_ref, b_ref, t_ref, z_ref, e_ref):
        e_ref[...] = (t_ref[...] + shifted(get_fine(b_ref), 2, 1)).T[:line_conts, :]
        put_coded(z_ref, [p_ref[...] + get_coded(a_ref, 1, width) + get_coded(b_ref, 0, width)])

    adj = (adj_t, other_t)
    (a3,) = backward("backward_3a", adj, [[(3, 3), (3, "a")]], [], us=1.5, fine=every, ready=ready)
    a3_got = send_first(a3)
    adj = (tie(adj_t, a3), other_t)
    a2, p3s, p3 = backward("backward_3b", adj, [[(2, 3), (2, "a")]], [(3, "b"), (3, 0)], us=3.3)
    a2_got = send_first(a2)
    adj = (tie(adj_t, a2), other_t)
    wanted = [(2, "b"), (2, 0), (1, "b"), (1, 0)]
    a1, p2s, p2, p1s, p1 = backward("backward_2", adj, [[(1, 3), (1, "a")]], wanted, us=3.5)
    b3, every = call(
        sum_3, [message(1, True), sds((scen, conts), F32)], [VM] * 3, "sum_3", us=0.3
    )(tie(p3s, a1), a3_got, every)
    b3_got = send_second(b3)
    adj = (tie(adj_t, b3), other_t)
    p0d, p0f, p0s, p0 = backward("backward_0", adj, [], [(0, 3), (0, "a"), (0, "b"), (0, 0)], us=3)
    z3, every = call(
        sum_z3, [message(1), sds((line_conts, scen), F32)], [VM] * 4, "sum_z3", us=0.3
    )(tie(p3, p0), a3_got, b3_got, every)
    every = every + send(every, 1) + send(every, 2) + send(every, 3)
    every = every + swap(every)
    a1_got = send_first(tie(a1, z3))
    z3_got = send(z3, 3)
    b2 = add("sum_2", tie(p2s, z3), (a2_got, 0))
    b2_got = send_second(b2)
    b1 = add("sum_1", tie(p1s, b2), (a1_got, 0))
    b1_got = send_second(b1)


    def outaged(d_ref, f_ref, p_ref, q_ref, e_ref, so_ref, out_ref, s_ref, o_ref, more):
        marks = so_ref[:, plane:].astype(F32)
        row = marks[:, :1] * 16.0 + marks[:, 1:2]
        wide = jnp.broadcast_to(row, (line_conts, LANES))
        across = jnp.concatenate([wide] * (LANES // line_conts), axis=0).T[:line_conts, :line_conts]
        one = lax.broadcasted_iota(jnp.int32, (line_conts, line_conts), 0)
        two = lax.broadcasted_iota(jnp.int32, (line_conts, line_conts), 1)
        same = (one // group == two // group) & (wide[:, :line_conts] == across)
        earlier = jnp.sum(jnp.where(same & (two < one), 1.0, 0.0), axis=1, keepdims=True)
        merged = pick(one_hot(same), e_ref[...])
        final = jnp.where(earlier > 0.0, 0.0, merged).astype(BF16)
        more[...] = lax.dot_general(final, so_ref[:, :plane], (((0,), (0,)), ((), ())), preferred_element_type=F32)

        def grad(ref, line):
            return ref[...] + more[:, at(spot_of(line), width)]

        put_coded(out_ref, [grad(d_ref, 3), grad(f_ref, "a")])
        s_ref[...] = grad(p_ref, "b")
        o_ref[...] = grad(q_ref, 0)

    a0, p0s, p0 = call(
        outaged, [message(2), grad_block, grad_block], [VM] * 6, "outaged_rows", [pltpu.VMEM((scen, plane), F32)], us=0.01
    )(tie(p0d, b1), p0f, p0s, p0, every, out_factors)
    a0_got = send_first(a0)

    def gather(p_ref, z3_ref, out_ref):
        out_ref[...] = p_ref[...] + get_coded(z3_ref, 0, width)

    p0 = call(gather, grad_block, [VM] * 2, "gradient_z", us=12)(tie(p0, a0), z3_got)
    z2 = add("sum_z2", tie(p2, a0), (a2_got, 1), (b2_got, 0))
    z2_got = send(z2, 2)
    z1 = add("sum_z1", tie(p1, z2, p0), (a1_got, 1), (b1_got, 0))
    z1_got = send(z1, 1)

    b0 = add("sum_0", tie(p0s, z1), (a0_got, 0))
    b0_got = send_second(b0)
    def last(p_ref, a_ref, b_ref, z1_ref, z2_ref, out_ref):
        total = p_ref[...] + get_coded(a_ref, 1, width)
        for ref in (b_ref, z2_ref, z1_ref):
            total = total + get_coded(ref, 0, width)
        out_ref[...] = total.T

    return call(last, sds((width, scen), F32), [VM] * 5, "gradient")(p0, a0_got, b0_got, z1_got, z2_got)


def on_device(
    shift_factors, injections, limits, entry_row, entry_owner, entry_slot, outage_factor, outage_row
):
    rows_group, bus_cols = shift_factors.shape
    br_count = lax.axis_size("br")
    bus_count = lax.axis_size("bus")
    rows_dev = rows_group // bus_count
    owned_conts = outage_row.shape[0]
    group_conts = owned_conts * bus_count
    factor_cols = shift_factors
    partial_flows = jnp.dot(
        factor_cols,
        lax.all_gather(injections, "br", axis=0, tiled=True),
        preferred_element_type=jnp.float32,
    )
    flows = lax.psum_scatter(partial_flows, "bus", scatter_dimension=0, tiled=True)
    limit_col = limits[:, None]
    base_adj = base_weight * (
        jnp.maximum(flows - limit_col, 0.0) + jnp.minimum(flows + limit_col, 0.0)
    )
    own_outage = jnp.take(flows, outage_row, axis=0)
    owner_ids = entry_owner[:, 0]
    all_outage = lax.all_gather(own_outage, ("br", "bus"), axis=0, tiled=True)
    contingency = owner_ids * group_conts + entry_slot
    fetched = jnp.take(all_outage, contingency, axis=0)
    post_flow = jnp.take(flows, entry_row, axis=0) + outage_factor[:, None] * fetched
    emerg_cap = emergency * jnp.take(limits, entry_row)[:, None]
    entry_adj = cont_weight * (
        jnp.maximum(post_flow - emerg_cap, 0.0) + jnp.minimum(post_flow + emerg_cap, 0.0)
    )
    weighted = outage_factor[:, None] * entry_adj
    local_rows = jnp.arange(rows_dev, dtype=jnp.int32)
    row_hot = (entry_row[:, None] == local_rows[None, :]).astype(jnp.float32)
    monitored_adj = lax.dot_general(
        row_hot,
        entry_adj,
        (((0,), (0,)), ((), ())),
        precision=lax.Precision.HIGHEST,
        preferred_element_type=jnp.float32,
    )
    every_part = jax.ops.segment_sum(
        weighted, contingency, num_segments=owned_conts * br_count * bus_count
    )
    owned_adj = lax.psum_scatter(every_part, ("br", "bus"), scatter_dimension=0, tiled=True)
    outage_hot = (outage_row[:, None] == local_rows[None, :]).astype(jnp.float32)
    outage_adj = lax.dot_general(
        outage_hot,
        owned_adj,
        (((0,), (0,)), ((), ())),
        precision=lax.Precision.HIGHEST,
        preferred_element_type=jnp.float32,
    )
    adjoint = (base_adj + monitored_adj + outage_adj).astype(jnp.bfloat16)
    group_adjoint = lax.all_gather(adjoint, "bus", axis=0, tiled=True)
    return lax.psum_scatter(
        lax.dot_general(
            factor_cols, group_adjoint, (((0,), (0,)), ((), ())), preferred_element_type=jnp.float32
        ),
        "br",
        scatter_dimension=0,
        tiled=True,
    )


def solution(mesh):
    in_specs = (
        P("br", "bus"),
        P(("bus", "br"), None),
        P(("br", "bus")),
        P(("br", "bus")),
        P(("br", "bus"), None),
        P(("br", "bus")),
        P(("br", "bus")),
        P(("br", "bus")),
    )
    out_specs = P(("bus", "br"), None)
    local = on_slice if (mesh.shape["br"], mesh.shape["bus"]) == (16, 2) else on_device
    return jax.shard_map(local, mesh=mesh, in_specs=in_specs, out_specs=out_specs, check_vma=False)
```
